128 devices in a mesh: sub: 8 (over x, core), slab: 16 (over y, z).
Axes of the slice: x: 4, y: 4, z: 4, core: 2. Of those that a mesh axis runs over, the one named last changes fastest.
Arguments:
- source: float32 [8, 256, 256, 256], P('sub', 'slab'), may hold values from -6 to 6
- coarse: float32 [2, 8, 256, 256, 256], P(None, 'sub', 'slab'), may hold values from -4 to 4
- rho: float32 [8], replicated, may hold values from 0.3 to 45, as said below
- basis_x: float32 [256, 256], replicated, may hold values from -0.375 to 0.375
- basis_y: float32 [256, 256], replicated, may hold values from -0.375 to 0.375
- basis_z: float32 [256, 256], replicated, may hold values from -0.375 to 0.375
- eigen_x: float32 [256], replicated, may hold values from 0.1 to 3
- eigen_y: float32 [256], replicated, may hold values from 0.1 to 3
- eigen_z: float32 [256], replicated, may hold values from 0.1 to 3
- face_stiff: float32 [256, 256], replicated, may hold values from 0.2 to 2
Outputs:
- solution: float32 [8, 256, 256, 256], P('sub', 'slab')
- multipliers: float32 [8, 256, 256], P('sub', 'slab')
- jump: float32 [8, 256, 256], P('sub', 'slab')
The draws below stay inside these ranges and needn't reach their ends.
Inputs may be any that keep to these rules, and one draw needn't show every extreme that they name: `rho`: positive coefficient of each subdomain.
All inputs are finite; a program needn't handle non-finite values.
Results may differ from the reference program's by a relative error of at most 0.00014.
Values sent between devices are 32-bit elements; how exact they have to be, the bound alone decides.
No kernel may reach another device: no remote copies, remote signals or barrier semaphores. Data moves between devices by JAX's collectives and lax.ppermute only.
A program may use at most 128 MiB of HBM per device.

```python
import math
import jax
import jax.numpy as jnp
from jax import lax

N = 256
ITERS = 2
SUBS = 8


def draw_rho(key, part):
    place = jnp.arange(SUBS, dtype=jnp.float32) / max(SUBS - 1, 1)
    jitter = jax.random.uniform(key, (SUBS,), jnp.float32, 0.7, 1.4)
    return jnp.exp(jnp.log(10.0) * place) * jitter


def steps_of(rng, shape, shards, low, top_value):
    factor_of, own = 1.0, jax.random.fold_in(rng, 6)
    for axis_at, shards_of in shards:
        draws = jnp.exp(jax.random.uniform(jax.random.fold_in(own, axis_at), (shards_of,), jnp.float32, low / len(shards), top_value / len(shards)))
        factor_of = factor_of * jnp.repeat(draws, shape[axis_at] // shards_of).reshape([-1 if axis == axis_at else 1 for axis in range(len(shape))])
    return factor_of


def scatter_about(stream_key, shape, scale, reach, split=(), kind=jnp.bfloat16):
    gain = steps_of(stream_key, shape, split, -0.22, 0.18) if split else 1.0
    result = jax.random.normal(stream_key, shape, jnp.float32) * scale * gain
    return jnp.minimum(jnp.maximum(result, -reach), reach).astype(kind)


def setup_inputs(seed: int = 0) -> dict:
    seeds = jax.random.split(jax.random.key(seed), 11)
    return {
        "source": scatter_about(seeds[0], (SUBS, N, N, N), 1.0, 6.0, ((0, 8), (1, 16)), jnp.float32),
        "coarse": scatter_about(seeds[1], (ITERS, SUBS, N, N, N), 0.5, 4.0, ((1, 8), (2, 16)), jnp.float32),
        "rho": draw_rho(jax.random.fold_in(seeds[10], 71), 0),
        "basis_x": scatter_about(seeds[3], (N, N), N ** -0.5, 0.375, (), jnp.float32),
        "basis_y": scatter_about(seeds[4], (N, N), N ** -0.5, 0.375, (), jnp.float32),
        "basis_z": scatter_about(seeds[5], (N, N), N ** -0.5, 0.375, (), jnp.float32),
        "eigen_x": jnp.clip(jnp.exp(jax.random.uniform(seeds[6], (N,), jnp.float32, math.log(0.1), math.log(3.0))), 0.1, 3.0),
        "eigen_y": jnp.clip(jnp.exp(jax.random.uniform(seeds[7], (N,), jnp.float32, math.log(0.1), math.log(3.0))), 0.1, 3.0),
        "eigen_z": jnp.clip(jnp.exp(jax.random.uniform(seeds[8], (N,), jnp.float32, math.log(0.1), math.log(3.0))), 0.1, 3.0),
        "face_stiff": jnp.clip(jnp.exp(jax.random.uniform(seeds[9], (N, N), jnp.float32, math.log(0.2), math.log(2.0))), 0.2, 2.0),
    }


HI = lax.Precision.HIGHEST


def forward(field, basis_x, basis_y, basis_z):
    part = jnp.einsum('xyz,zk->xyk', field, basis_z, precision=HI)
    part = jnp.einsum('xyk,yj->xjk', part, basis_y, precision=HI)
    return jnp.einsum('xjk,xi->ijk', part, basis_x, precision=HI)


def inverse(modes, basis_x, basis_y, basis_z):
    part = jnp.einsum('ijk,xi->xjk', modes, basis_x, precision=HI)
    part = jnp.einsum('xjk,yj->xyk', part, basis_y, precision=HI)
    return jnp.einsum('xyk,zk->xyz', part, basis_z, precision=HI)


def reference(source, coarse, rho, basis_x, basis_y, basis_z, eigen_x, eigen_y, eigen_z, face_stiff):
    denom = eigen_x[:, None, None] + eigen_y[None, :, None] + eigen_z[None, None, :]

    def solve_one(pair):
        field, coeff = pair
        modes = forward(field, basis_x, basis_y, basis_z) / (denom * coeff)
        return inverse(modes, basis_x, basis_y, basis_z)

    weights = 0.5 * (rho + jnp.roll(rho, -1))
    multipliers = jnp.zeros((SUBS, N, N), jnp.float32)
    solution = source
    jump = multipliers
    for step in range(ITERS):
        earlier = jnp.roll(multipliers, 1, axis=0)
        load = source + coarse[step]
        load = load.at[:, :, :, N - 1].add(-multipliers)
        load = load.at[:, :, :, 0].add(earlier)
        solution = lax.map(solve_one, (load, rho))
        jump = solution[:, :, :, N - 1] - jnp.roll(solution[:, :, :, 0], -1, axis=0)
        face = jnp.einsum('sxy,yj->sxj', jump, basis_y, precision=HI)
        face = jnp.einsum('sxj,xi->sij', face, basis_x, precision=HI)
        face = face * face_stiff[None]
        face = jnp.einsum('sij,xi->sxj', face, basis_x, precision=HI)
        face = jnp.einsum('sxj,yj->sxy', face, basis_y, precision=HI)
        search = weights[:, None, None] * face
        alpha = jnp.sum(jump * search) / (jnp.sum(search * search) + 1e-6)
        multipliers = multipliers + alpha * search
    return solution, multipliers, jump
```

```python
import functools

import jax
import jax.numpy as jnp
from jax import lax
from jax.experimental import pallas as pl
from jax.experimental.pallas import tpu as pltpu
from jax.sharding import PartitionSpec as P

HI = lax.Precision.HIGHEST
F32 = jnp.float32
BF16 = jnp.bfloat16
VMEM_LIMIT = 48 * 1024 * 1024
N = 256
ROWS = 16
SLABS = 16
LANES = 128
FIELD = (SLABS, 2, N // SLABS, ROWS, LANES)


def params():
    return pltpu.CompilerParams(vmem_limit_bytes=VMEM_LIMIT)


def split(a):
    high = a.astype(BF16)
    low = (a - high.astype(F32)).astype(BF16)
    return high, low


def dot(a, b):
    return jnp.dot(a, b, preferred_element_type=F32)


def dot3(a, b):
    return dot(a[0], b[0]) + (dot(a[0], b[1]) + dot(a[1], b[0]))


def put_split(scratch, a):
    scratch[0], scratch[1] = split(a)


def whole(shape):
    return pl.BlockSpec(shape, lambda *_: (0,) * len(shape))


def smem():
    return pl.BlockSpec(memory_space=pltpu.SMEM)


def forward_kernel(source, coarse, basis_y, basis_z, out, left, right):
    x = pl.program_id(0)

    @pl.when(x == 0)
    def _():
        put_split(left, basis_y[...].T)
        put_split(right, basis_z[...])

    load = source[0] + coarse[0, 0, 0]
    part = dot3(split(load), right)
    part = dot3(left, split(part))
    for slab in range(SLABS):
        for half in range(2):
            rows = out.at[slab, half].reshape(ROWS * 8, LANES)
            piece = part[slab * ROWS : slab * ROWS + ROWS, LANES * half : LANES * half + LANES]
            rows[pl.ds(x % 8, ROWS, stride=8), :] = piece


def forward(source, coarse, step, basis_y, basis_z):
    return pl.pallas_call(
        forward_kernel,
        grid=(ROWS,),
        in_specs=[
            pl.BlockSpec((1, N, N), lambda x: (x, 0, 0)),
            pl.BlockSpec((1, 1, 1, N, N), lambda x: (step, 0, x, 0, 0)),
            whole((N, N)),
            whole((N, N)),
        ],
        out_specs=pl.BlockSpec((SLABS, 2, ROWS, 8, LANES), lambda x: (0, 0, 0, x // 8, 0)),
        out_shape=jax.ShapeDtypeStruct(FIELD, F32),
        scratch_shapes=[pltpu.VMEM((2, N, N), BF16), pltpu.VMEM((2, N, N), BF16)],
        compiler_params=params(),
        cost_estimate=pl.CostEstimate(
            flops=12 * ROWS * N**3, bytes_accessed=12 * ROWS * N * N, transcendentals=0
        ),
        name="forward",
    )(source, coarse, basis_y, basis_z)


def middle_kernel(base, shift, basis_x, lines, out, left, right):
    j = pl.program_id(0)

    @pl.when(j == 0)
    def _():
        put_split(left, basis_x[...].T)
        put_split(right, basis_x[...])

    field = jnp.concatenate([lines[:, half, 0].reshape(N, LANES) for half in range(2)], axis=1)
    modes = dot3(left, split(field)) / (base[...] + shift[j])
    spread = dot3(right, split(modes))
    for half in range(2):
        piece = spread[:, LANES * half : LANES * half + LANES]
        out[:, half, 0] = piece.reshape(SLABS, ROWS, LANES)


def middle(base, shift, basis_x, lines):
    block = pl.BlockSpec((SLABS, 2, 1, ROWS, LANES), lambda j: (0, 0, j, 0, 0))
    return pl.pallas_call(
        middle_kernel,
        grid=(N // SLABS,),
        in_specs=[whole((N, N)), smem(), whole((N, N)), block],
        out_specs=block,
        out_shape=jax.ShapeDtypeStruct(FIELD, F32),
        scratch_shapes=[pltpu.VMEM((2, N, N), BF16), pltpu.VMEM((2, N, N), BF16)],
        compiler_params=params(),
        cost_estimate=pl.CostEstimate(
            flops=12 * ROWS * N**3, bytes_accessed=8 * ROWS * N * N, transcendentals=0
        ),
        name="middle",
    )(base, shift, basis_x, lines)


def backward_kernel(field, extra, basis_y, basis_z, out, left, right):
    x = pl.program_id(0)

    @pl.when(x == 0)
    def _():
        put_split(left, basis_y[...])
        put_split(right, basis_z[...].T)

    def rows(ref, slab, half):
        return ref.at[slab, half].reshape(ROWS * 8, LANES)[pl.ds(x % 8, ROWS, stride=8), :]

    halves = [
        jnp.concatenate(
            [rows(field, slab, half) + rows(extra, slab, half) for slab in range(SLABS)], axis=0
        )
        for half in range(2)
    ]
    part = dot3(left, split(jnp.concatenate(halves, axis=1)))
    out[0] = dot3(split(part), right)


def backward(field, extra, basis_y, basis_z):
    block = pl.BlockSpec((SLABS, 2, ROWS, 8, LANES), lambda x: (0, 0, 0, x // 8, 0))
    return pl.pallas_call(
        backward_kernel,
        grid=(ROWS,),
        in_specs=[block, block, whole((N, N)), whole((N, N))],
        out_specs=pl.BlockSpec((1, N, N), lambda x: (x, 0, 0)),
        out_shape=jax.ShapeDtypeStruct((ROWS, N, N), F32),
        scratch_shapes=[pltpu.VMEM((2, N, N), BF16), pltpu.VMEM((2, N, N), BF16)],
        compiler_params=params(),
        cost_estimate=pl.CostEstimate(
            flops=12 * ROWS * N**3, bytes_accessed=12 * ROWS * N * N, transcendentals=0
        ),
        name="backward",
    )(field, extra, basis_y, basis_z)


def inverse_parts(denom):
    high = pl.reciprocal(denom, approx=True).astype(BF16)
    wide = high.astype(F32)
    low = (wide * (1.0 - denom * wide)).astype(BF16)
    return high, low


def times_inverse(rows, denom):
    high, low = split(rows)
    count = rows.shape[0]
    w_high, w_low = inverse_parts(denom)
    both = dot(jnp.concatenate([high, low], axis=0), w_high)
    return both[:count] + (both[count:] + dot(high, w_low))


def faces_kernel(base, shift, own_x, ends, products, part0, part1, out):
    block = pl.program_id(0)
    first, last = ends[0:1], ends[1:2]
    for jj in range(8):
        a = jnp.concatenate([part0[0, 0, jj], part0[0, 1, jj]], axis=1)
        b = jnp.concatenate([part1[0, 0, jj], part1[0, 1, jj]], axis=1)
        rows = jnp.concatenate([a * last, b * last, a * first, b * first, products[...]], axis=0)
        result = times_inverse(rows, base[...] + shift[block * 8 + jj])
        for face in range(4):
            piece = result[16 * face : 16 * face + 16] * own_x[...]
            out[0, face, jj : jj + 1] = jnp.sum(piece, axis=0, keepdims=True)
        for pair in range(3):
            out[0, 4 + pair, jj : jj + 1] = result[64 + pair : 65 + pair]


def faces(base, shift, own_x, ends, products, part0, part1):
    block = pl.BlockSpec((1, 2, 8, ROWS, LANES), lambda j: (j // 2, 0, j % 2, 0, 0))
    return pl.pallas_call(
        faces_kernel,
        grid=(N // 8,),
        in_specs=[
            whole((N, N)),
            smem(),
            whole((ROWS, N)),
            whole((2, N)),
            whole((16, N)),
            block,
            block,
        ],
        out_specs=pl.BlockSpec((1, 7, 8, N), lambda j: (j // 2, 0, j % 2, 0)),
        out_shape=jax.ShapeDtypeStruct((SLABS, 7, N // SLABS, N), F32),
        compiler_params=params(),
        cost_estimate=pl.CostEstimate(
            flops=2 * 1000 * N**3, bytes_accessed=8 * ROWS * N * N, transcendentals=N**3
        ),
        name="faces",
    )(base, shift, own_x, ends, products, part0, part1)


def extra_kernel(base, shift, own_x, ends, faces_in, out):
    block = pl.program_id(0)
    first, last = ends[0:1], ends[1:2]
    for jj in range(8):
        upper = own_x[...] * faces_in[0, jj : jj + 1]
        lower = own_x[...] * faces_in[1, jj : jj + 1]
        rows = jnp.concatenate([upper, lower], axis=0)
        result = times_inverse(rows, base[...] + shift[block * 8 + jj])
        result = first * result[16:] - last * result[:16]
        for half in range(2):
            out[0, half, jj] = result[:, LANES * half : LANES * half + LANES]


def extra(base, shift, own_x, ends, faces_in):
    return pl.pallas_call(
        extra_kernel,
        grid=(N // 8,),
        in_specs=[
            whole((N, N)),
            smem(),
            whole((ROWS, N)),
            whole((2, N)),
            pl.BlockSpec((2, 8, N), lambda j: (0, j, 0)),
        ],
        out_specs=pl.BlockSpec((1, 2, 8, ROWS, LANES), lambda j: (j // 2, 0, j % 2, 0, 0)),
        out_shape=jax.ShapeDtypeStruct(FIELD, F32),
        compiler_params=params(),
        cost_estimate=pl.CostEstimate(
            flops=2 * 1000 * N**3, bytes_accessed=4 * ROWS * N * N, transcendentals=N**3
        ),
        name="extra",
    )(base, shift, own_x, ends, faces_in)


def exact(a, b):
    return jnp.dot(a, b, precision=HI, preferred_element_type=F32)


def exact_t(a, b):
    dims = (((1,), (1,)), ((), ()))
    return lax.dot_general(a, b, dims, precision=HI, preferred_element_type=F32)


def precondition(jump, gram_x, gram_y, stiff):
    seen = exact(exact(gram_y, jump), gram_x)
    search = stiff * seen
    image = exact(exact(gram_y, search), gram_x)
    return search, image, jnp.sum(seen * search), jnp.sum(image * search)


def scalars_block(upper, lower):
    at = lax.broadcasted_iota(jnp.int32, (8, 128), 0)
    return jnp.where(at == 0, upper, jnp.where(at == 1, lower, 0.0))


def chain0_kernel(jump, gram_x, gram_y, stiff, search, image, sums):
    search[...], image[...], upper, lower = precondition(
        jump[...], gram_x[...], gram_y[...], stiff[...]
    )
    sums[...] = scalars_block(upper, lower)


def chain0(jump, gram_x, gram_y, stiff):
    face = jax.ShapeDtypeStruct((N, N), F32)
    return pl.pallas_call(
        chain0_kernel,
        out_shape=(face, face, jax.ShapeDtypeStruct((8, 128), F32)),
        compiler_params=params(),
        cost_estimate=pl.CostEstimate(
            flops=48 * N**3, bytes_accessed=24 * N * N, transcendentals=0
        ),
        name="chain0",
    )(jump, gram_x, gram_y, stiff)


def chain1_kernel(
    scale, jump, image, before, after, table, gram_x, gram_y, stiff, own_x, basis_y, search, sums, out
):
    alpha, ratio = scale[0], scale[1]
    t = image[...]
    own = table[1] * before[...] - table[0] * t
    other = table[2] * t - table[1] * after[...]
    q = jump[...] + alpha * (own - ratio * other)
    search[...], _, upper, lower = precondition(q, gram_x[...], gram_y[...], stiff[...])
    sums[...] = scalars_block(upper, lower)
    out[...] = exact_t(exact_t(own_x[...], q), basis_y[...])


def chain1(*args):
    return pl.pallas_call(
        chain1_kernel,
        in_specs=[smem()] + [pl.BlockSpec(memory_space=pltpu.VMEM)] * 10,
        out_shape=(
            jax.ShapeDtypeStruct((N, N), F32),
            jax.ShapeDtypeStruct((8, 128), F32),
            jax.ShapeDtypeStruct((ROWS, N), F32),
        ),
        compiler_params=params(),
        cost_estimate=pl.CostEstimate(
            flops=50 * N**3, bytes_accessed=48 * N * N, transcendentals=0
        ),
        name="chain1",
    )(*args)


def final_kernel(scale, search0, search1, own_x, basis_y, out):
    total = scale[0] * search0[...] + scale[1] * search1[...]
    out[...] = exact_t(exact_t(own_x[...], total), basis_y[...])


def final(*args):
    return pl.pallas_call(
        final_kernel,
        in_specs=[smem()] + [pl.BlockSpec(memory_space=pltpu.VMEM)] * 4,
        out_shape=jax.ShapeDtypeStruct((ROWS, N), F32),
        compiler_params=params(),
        name="final",
    )(*args)


def gram_kernel(basis_x, basis_y, gram_x, gram_y):
    gram_x[...] = exact(basis_x[...].T, basis_x[...])
    gram_y[...] = exact(basis_y[...].T, basis_y[...])


def grams(basis_x, basis_y):
    face = jax.ShapeDtypeStruct((N, N), F32)
    return pl.pallas_call(
        gram_kernel, out_shape=(face, face), compiler_params=params(), name="grams"
    )(basis_x, basis_y)


def from_behind(block, axis, distance):
    count = lax.axis_size(axis)
    route = [((i - distance) % count, i) for i in range(count)]
    return lax.ppermute(block, axis, route)


def sum_over_subs(sums):
    for bit in (1, 2, 4):
        sums = sums + lax.ppermute(sums, "sub", [(i, i ^ bit) for i in range(8)])
    return sums


def step_length(sums):
    return sums[0, 0] / (sums[1, 0] + 1e-06)


def exchange(block):
    return lax.all_to_all(block, "slab", split_axis=0, concat_axis=0, tiled=True)


def on_device(
    source, coarse, rho, basis_x, basis_y, basis_z, eigen_x, eigen_y, eigen_z, face_stiff
):
    source = source[0]
    sub_index = lax.axis_index("sub")
    slab_index = lax.axis_index("slab")
    subs = lax.axis_size("sub")
    own_rho = lax.dynamic_slice_in_dim(rho, sub_index, 1, 0)[0]
    next_rho = lax.dynamic_slice_in_dim(rho, (sub_index + 1) % subs, 1, 0)[0]
    weight = 0.5 * (own_rho + next_rho)
    start = slab_index * ROWS
    own_x = lax.dynamic_slice_in_dim(basis_x, start, ROWS, 0)

    part1 = forward(source, coarse, 1, basis_y, basis_z)
    lines = exchange(part1)

    base_xz = own_rho * (eigen_x[:, None] + eigen_z[None, :])
    base_zx = own_rho * (eigen_z[:, None] + eigen_x[None, :])
    shift = own_rho * eigen_y
    own_shift = lax.dynamic_slice_in_dim(shift, start, ROWS, 0)
    ends = jnp.stack([basis_z[0], basis_z[N - 1]])
    products = jnp.stack([ends[1] * ends[1], ends[1] * ends[0], ends[0] * ends[0]])
    products = jnp.pad(products, ((0, 13), (0, 0)))
    stiff = weight * face_stiff.T
    gram_x, gram_y = grams(basis_x, basis_y)

    part0 = forward(source, coarse, 0, basis_y, basis_z)
    pieces = faces(base_zx, shift, own_x, ends, products, part0, part1)
    table = pieces[:, 4:].transpose(1, 0, 2, 3).reshape(3, N, N)
    following = from_behind(pieces[:, 2:4], "sub", -1)
    shares = exchange(pieces[:, 0:2] - following)
    jumps = jnp.sum(shares, axis=0)
    jumps = exchange(jnp.broadcast_to(jumps[None], (SLABS,) + jumps.shape))
    jumps = jumps.transpose(1, 0, 2, 3).reshape(2, N, N)

    search0, image0, sums0 = chain0(jumps[0], gram_x, gram_y, stiff)
    before = from_behind(image0, "sub", 1)
    after = from_behind(image0, "sub", -1)
    alpha0 = step_length(sum_over_subs(sums0))

    spread = exchange(middle(base_xz, own_shift, basis_x, lines))

    more = extra(base_xz, shift, own_x, ends, alpha0 * jnp.stack([image0, before]))
    scale = jnp.stack([alpha0, own_rho / next_rho])
    search1, sums1, jump = chain1(
        scale, jumps[1], image0, before, after, table, gram_x, gram_y, stiff, own_x, basis_y
    )
    alpha1 = step_length(sum_over_subs(sums1))
    multipliers = final(jnp.stack([alpha0, alpha1]), search0, search1, own_x, basis_y)
    solution = backward(spread, more, basis_y, basis_z)
    return (solution[None], multipliers[None], jump[None])


def solution(mesh):
    in_specs = (
        P("sub", "slab", None, None),
        P(None, "sub", "slab", None, None),
        P(),
        P(),
        P(),
        P(),
        P(),
        P(),
        P(),
        P(),
    )
    out_specs = (P("sub", "slab", None, None), P("sub", "slab", None), P("sub", "slab", None))
    return jax.shard_map(
        on_device, mesh=mesh, in_specs=in_specs, out_specs=out_specs, check_vma=False
    )
```

```python
import functools

import jax
import jax.numpy as jnp
from jax import lax
from jax.experimental import pallas as pl
from jax.experimental.pallas import tpu as pltpu
from jax.sharding import PartitionSpec as P

HI = lax.Precision.HIGHEST
F32 = jnp.float32
BF16 = jnp.bfloat16
VMEM_LIMIT = 48 * 1024 * 1024
N = 256
ROWS = 16
SLABS = 16
LANES = 128
GROUP = 4
FIELD = (SLABS, 2, N // SLABS, ROWS, LANES)


def params():
    return pltpu.CompilerParams(vmem_limit_bytes=VMEM_LIMIT)


def split(a):
    high = a.astype(BF16)
    low = (a - high.astype(F32)).astype(BF16)
    return high, low


def dot(a, b):
    return jnp.dot(a, b, preferred_element_type=F32)


def dot3(a, b):
    return dot(a[0], b[0]) + (dot(a[0], b[1]) + dot(a[1], b[0]))


def put_split(scratch, a):
    scratch[0], scratch[1] = split(a)


def whole(shape):
    return pl.BlockSpec(shape, lambda *_: (0,) * len(shape))


def smem():
    return pl.BlockSpec(memory_space=pltpu.SMEM)


def forward_kernel(source, coarse, basis_y, basis_z, out, left, right):
    step = pl.program_id(0)

    @pl.when(step == 0)
    def _():
        put_split(left, basis_y[...].T)
        put_split(right, basis_z[...])

    load = (source[...] + coarse[0, 0]).reshape(GROUP * N, N)
    first = dot3(split(load), right)
    for x in range(GROUP):
        part = dot3(left, split(first[x * N : x * N + N]))
        at = pl.ds((step * GROUP + x) % 8, ROWS, stride=8)
        for slab in range(SLABS):
            for half in range(2):
                rows = out.at[slab, half].reshape(ROWS * 8, LANES)
                piece = part[slab * ROWS : slab * ROWS + ROWS, LANES * half : LANES * half + LANES]
                rows[at, :] = piece


def forward(source, coarse, step, basis_y, basis_z):
    return pl.pallas_call(
        forward_kernel,
        grid=(ROWS // GROUP,),
        in_specs=[
            pl.BlockSpec((GROUP, N, N), lambda x: (x, 0, 0)),
            pl.BlockSpec((1, 1, GROUP, N, N), lambda x: (step, 0, x, 0, 0)),
            whole((N, N)),
            whole((N, N)),
        ],
        out_specs=pl.BlockSpec(
            (SLABS, 2, ROWS, 8, LANES), lambda x: (0, 0, 0, x * GROUP // 8, 0)
        ),
        out_shape=jax.ShapeDtypeStruct(FIELD, F32),
        scratch_shapes=[pltpu.VMEM((2, N, N), BF16), pltpu.VMEM((2, N, N), BF16)],
        compiler_params=params(),
        cost_estimate=pl.CostEstimate(
            flops=12 * ROWS * N**3, bytes_accessed=12 * ROWS * N * N, transcendentals=0
        ),
        name="forward",
    )(source, coarse, basis_y, basis_z)


def middle_kernel(base, shift, basis_x, lines, out, left, right):
    step = pl.program_id(0)

    @pl.when(step == 0)
    def _():
        put_split(left, basis_x[...].T)
        put_split(right, basis_x[...])

    for j in range(GROUP):
        halves = [lines[:, half, j].reshape(N, LANES) for half in range(2)]
        field = jnp.concatenate(halves, axis=1)
        modes = dot3(left, split(field)) / (base[...] + shift[step * GROUP + j])
        spread = dot3(right, split(modes))
        for half in range(2):
            piece = spread[:, LANES * half : LANES * half + LANES]
            out[:, half, j] = piece.reshape(SLABS, ROWS, LANES)


def middle(base, shift, basis_x, lines):
    block = pl.BlockSpec((SLABS, 2, GROUP, ROWS, LANES), lambda j: (0, 0, j, 0, 0))
    return pl.pallas_call(
        middle_kernel,
        grid=(N // SLABS // GROUP,),
        in_specs=[whole((N, N)), smem(), whole((N, N)), block],
        out_specs=block,
        out_shape=jax.ShapeDtypeStruct(FIELD, F32),
        scratch_shapes=[pltpu.VMEM((2, N, N), BF16), pltpu.VMEM((2, N, N), BF16)],
        compiler_params=params(),
        cost_estimate=pl.CostEstimate(
            flops=12 * ROWS * N**3, bytes_accessed=8 * ROWS * N * N, transcendentals=0
        ),
        name="middle",
    )(base, shift, basis_x, lines)


def backward_kernel(field, extra, basis_y, basis_z, out, left, right):
    step = pl.program_id(0)

    @pl.when(step == 0)
    def _():
        put_split(left, basis_y[...])
        put_split(right, basis_z[...].T)

    def total(x, slab, half):
        at = pl.ds((step * GROUP + x) % 8, ROWS, stride=8)
        terms = [ref.at[slab, half].reshape(ROWS * 8, LANES)[at, :] for ref in (field, extra)]
        return terms[0] + terms[1]

    parts = []
    for x in range(GROUP):
        halves = [
            jnp.concatenate([total(x, slab, half) for slab in range(SLABS)], axis=0)
            for half in range(2)
        ]
        parts.append(dot3(left, split(jnp.concatenate(halves, axis=1))))
    part = jnp.concatenate(parts, axis=0)
    out[...] = dot3(split(part), right).reshape(GROUP, N, N)


def backward(field, extra, basis_y, basis_z):
    block = pl.BlockSpec((SLABS, 2, ROWS, 8, LANES), lambda x: (0, 0, 0, x * GROUP // 8, 0))
    return pl.pallas_call(
        backward_kernel,
        grid=(ROWS // GROUP,),
        in_specs=[block, block, whole((N, N)), whole((N, N))],
        out_specs=pl.BlockSpec((GROUP, N, N), lambda x: (x, 0, 0)),
        out_shape=jax.ShapeDtypeStruct((ROWS, N, N), F32),
        scratch_shapes=[pltpu.VMEM((2, N, N), BF16), pltpu.VMEM((2, N, N), BF16)],
        compiler_params=params(),
        cost_estimate=pl.CostEstimate(
            flops=12 * ROWS * N**3, bytes_accessed=12 * ROWS * N * N, transcendentals=0
        ),
        name="backward",
    )(field, extra, basis_y, basis_z)


def inverse_parts(denom):
    high = pl.reciprocal(denom, approx=True).astype(BF16)
    wide = high.astype(F32)
    low = (wide * (1.0 - denom * wide)).astype(BF16)
    return high, low


def times_inverse(rows, denom):
    high, low = split(rows)
    count = rows.shape[0]
    w_high, w_low = inverse_parts(denom)
    both = dot(jnp.concatenate([high, low], axis=0), w_high)
    return both[:count] + (both[count:] + dot(high, w_low))


def faces_kernel(base, shift, own_x, ends, products, part0, part1, out):
    block = pl.program_id(0)
    first, last = ends[0:1], ends[1:2]
    for jj in range(8):
        a = jnp.concatenate([part0[0, 0, jj], part0[0, 1, jj]], axis=1)
        b = jnp.concatenate([part1[0, 0, jj], part1[0, 1, jj]], axis=1)
        rows = jnp.concatenate([a * last, b * last, a * first, b * first, products[...]], axis=0)
        result = times_inverse(rows, base[...] + shift[block * 8 + jj])
        for face in range(4):
            piece = result[16 * face : 16 * face + 16] * own_x[...]
            out[0, face, jj : jj + 1] = jnp.sum(piece, axis=0, keepdims=True)
        for pair in range(3):
            out[0, 4 + pair, jj : jj + 1] = result[64 + pair : 65 + pair]


def faces(base, shift, own_x, ends, products, part0, part1):
    block = pl.BlockSpec((1, 2, 8, ROWS, LANES), lambda j: (j // 2, 0, j % 2, 0, 0))
    return pl.pallas_call(
        faces_kernel,
        grid=(N // 8,),
        in_specs=[
            whole((N, N)),
            smem(),
            whole((ROWS, N)),
            whole((2, N)),
            whole((16, N)),
            block,
            block,
        ],
        out_specs=pl.BlockSpec((1, 7, 8, N), lambda j: (j // 2, 0, j % 2, 0)),
        out_shape=jax.ShapeDtypeStruct((SLABS, 7, N // SLABS, N), F32),
        compiler_params=params(),
        cost_estimate=pl.CostEstimate(
            flops=2 * 1000 * N**3, bytes_accessed=8 * ROWS * N * N, transcendentals=N**3
        ),
        name="faces",
    )(base, shift, own_x, ends, products, part0, part1)


def extra_kernel(base, shift, own_x, ends, faces_in, out):
    block = pl.program_id(0)
    first, last = ends[0:1], ends[1:2]
    for jj in range(8):
        upper = own_x[...] * faces_in[0, jj : jj + 1]
        lower = own_x[...] * faces_in[1, jj : jj + 1]
        rows = jnp.concatenate([upper, lower], axis=0)
        result = times_inverse(rows, base[...] + shift[block * 8 + jj])
        result = first * result[16:] - last * result[:16]
        for half in range(2):
            out[0, half, jj] = result[:, LANES * half : LANES * half + LANES]


def extra(base, shift, own_x, ends, faces_in):
    return pl.pallas_call(
        extra_kernel,
        grid=(N // 8,),
        in_specs=[
            whole((N, N)),
            smem(),
            whole((ROWS, N)),
            whole((2, N)),
            pl.BlockSpec((2, 8, N), lambda j: (0, j, 0)),
        ],
        out_specs=pl.BlockSpec((1, 2, 8, ROWS, LANES), lambda j: (j // 2, 0, j % 2, 0, 0)),
        out_shape=jax.ShapeDtypeStruct(FIELD, F32),
        compiler_params=params(),
        cost_estimate=pl.CostEstimate(
            flops=2 * 1000 * N**3, bytes_accessed=4 * ROWS * N * N, transcendentals=N**3
        ),
        name="extra",
    )(base, shift, own_x, ends, faces_in)


def exact(a, b):
    return jnp.dot(a, b, precision=HI, preferred_element_type=F32)


def exact_t(a, b):
    dims = (((1,), (1,)), ((), ()))
    return lax.dot_general(a, b, dims, precision=HI, preferred_element_type=F32)


def precondition(jump, gram_x, gram_y, stiff):
    seen = exact(exact(gram_y, jump), gram_x)
    search = stiff * seen
    image = exact(exact(gram_y, search), gram_x)
    return search, image, jnp.sum(seen * search), jnp.sum(image * search)


def scalars_block(upper, lower):
    at = lax.broadcasted_iota(jnp.int32, (8, 128), 0)
    return jnp.where(at == 0, upper, jnp.where(at == 1, lower, 0.0))


def chain0_kernel(jump, gram_x, gram_y, stiff, search, image, sums):
    search[...], image[...], upper, lower = precondition(
        jump[...], gram_x[...], gram_y[...], stiff[...]
    )
    sums[...] = scalars_block(upper, lower)


def chain0(jump, gram_x, gram_y, stiff):
    face = jax.ShapeDtypeStruct((N, N), F32)
    return pl.pallas_call(
        chain0_kernel,
        out_shape=(face, face, jax.ShapeDtypeStruct((8, 128), F32)),
        compiler_params=params(),
        cost_estimate=pl.CostEstimate(
            flops=48 * N**3, bytes_accessed=24 * N * N, transcendentals=0
        ),
        name="chain0",
    )(jump, gram_x, gram_y, stiff)


def chain1_kernel(
    scale, jump, image, before, after, table, gram_x, gram_y, stiff, own_x, basis_y, search, sums, out
):
    alpha, ratio = scale[0], scale[1]
    t = image[...]
    own = table[1] * before[...] - table[0] * t
    other = table[2] * t - table[1] * after[...]
    q = jump[...] + alpha * (own - ratio * other)
    search[...], _, upper, lower = precondition(q, gram_x[...], gram_y[...], stiff[...])
    sums[...] = scalars_block(upper, lower)
    out[...] = exact_t(exact_t(own_x[...], q), basis_y[...])


def chain1(*args):
    return pl.pallas_call(
        chain1_kernel,
        in_specs=[smem()] + [pl.BlockSpec(memory_space=pltpu.VMEM)] * 10,
        out_shape=(
            jax.ShapeDtypeStruct((N, N), F32),
            jax.ShapeDtypeStruct((8, 128), F32),
            jax.ShapeDtypeStruct((ROWS, N), F32),
        ),
        compiler_params=params(),
        cost_estimate=pl.CostEstimate(
            flops=50 * N**3, bytes_accessed=48 * N * N, transcendentals=0
        ),
        name="chain1",
    )(*args)


def final_kernel(scale, search0, search1, own_x, basis_y, out):
    total = scale[0] * search0[...] + scale[1] * search1[...]
    out[...] = exact_t(exact_t(own_x[...], total), basis_y[...])


def final(*args):
    return pl.pallas_call(
        final_kernel,
        in_specs=[smem()] + [pl.BlockSpec(memory_space=pltpu.VMEM)] * 4,
        out_shape=jax.ShapeDtypeStruct((ROWS, N), F32),
        compiler_params=params(),
        name="final",
    )(*args)


def gram_kernel(basis_x, basis_y, gram_x, gram_y):
    gram_x[...] = exact(basis_x[...].T, basis_x[...])
    gram_y[...] = exact(basis_y[...].T, basis_y[...])


def grams(basis_x, basis_y):
    face = jax.ShapeDtypeStruct((N, N), F32)
    return pl.pallas_call(
        gram_kernel, out_shape=(face, face), compiler_params=params(), name="grams"
    )(basis_x, basis_y)


def from_behind(block, axis, distance):
    count = lax.axis_size(axis)
    route = [((i - distance) % count, i) for i in range(count)]
    return lax.ppermute(block, axis, route)


def sum_over_subs(sums):
    for bit in (1, 2, 4):
        sums = sums + lax.ppermute(sums, "sub", [(i, i ^ bit) for i in range(8)])
    return sums


def step_length(sums):
    return sums[0, 0] / (sums[1, 0] + 1e-06)


def exchange(block):
    return lax.all_to_all(block, "slab", split_axis=0, concat_axis=0, tiled=True)


def on_device(
    source, coarse, rho, basis_x, basis_y, basis_z, eigen_x, eigen_y, eigen_z, face_stiff
):
    source = source[0]
    sub_index = lax.axis_index("sub")
    slab_index = lax.axis_index("slab")
    subs = lax.axis_size("sub")
    own_rho = lax.dynamic_slice_in_dim(rho, sub_index, 1, 0)[0]
    next_rho = lax.dynamic_slice_in_dim(rho, (sub_index + 1) % subs, 1, 0)[0]
    weight = 0.5 * (own_rho + next_rho)
    start = slab_index * ROWS
    own_x = lax.dynamic_slice_in_dim(basis_x, start, ROWS, 0)

    part1 = forward(source, coarse, 1, basis_y, basis_z)
    lines = exchange(part1)

    base_xz = own_rho * (eigen_x[:, None] + eigen_z[None, :])
    base_zx = own_rho * (eigen_z[:, None] + eigen_x[None, :])
    shift = own_rho * eigen_y
    own_shift = lax.dynamic_slice_in_dim(shift, start, ROWS, 0)
    ends = jnp.stack([basis_z[0], basis_z[N - 1]])
    products = jnp.stack([ends[1] * ends[1], ends[1] * ends[0], ends[0] * ends[0]])
    products = jnp.pad(products, ((0, 13), (0, 0)))
    stiff = weight * face_stiff.T
    gram_x, gram_y = grams(basis_x, basis_y)

    part0 = forward(source, coarse, 0, basis_y, basis_z)
    pieces = faces(base_zx, shift, own_x, ends, products, part0, part1)
    table = pieces[:, 4:].transpose(1, 0, 2, 3).reshape(3, N, N)
    following = from_behind(pieces[:, 2:4], "sub", -1)
    pieces, following, lines = lax.optimization_barrier((pieces, following, lines))
    shares = exchange(pieces[:, 0:2] - following)
    own_jumps = jnp.sum(shares, axis=0)
    jumps = exchange(jnp.broadcast_to(own_jumps[None], (SLABS,) + own_jumps.shape))
    jumps = jumps.transpose(1, 0, 2, 3).reshape(2, N, N)

    spread = middle(base_xz, own_shift, basis_x, lines)
    spread, jumps = lax.optimization_barrier((spread, jumps))
    spread = exchange(spread)

    search0, image0, sums0 = chain0(jumps[0], gram_x, gram_y, stiff)
    before = from_behind(image0, "sub", 1)
    after = from_behind(image0, "sub", -1)
    alpha0 = step_length(sum_over_subs(sums0))

    more = extra(base_xz, shift, own_x, ends, alpha0 * jnp.stack([image0, before]))
    scale = jnp.stack([alpha0, own_rho / next_rho])
    search1, sums1, jump = chain1(
        scale, jumps[1], image0, before, after, table, gram_x, gram_y, stiff, own_x, basis_y
    )
    alpha1 = step_length(sum_over_subs(sums1))
    multipliers = final(jnp.stack([alpha0, alpha1]), search0, search1, own_x, basis_y)
    solution = backward(spread, more, basis_y, basis_z)
    return (solution[None], multipliers[None], jump[None])


def solution(mesh):
    in_specs = (
        P("sub", "slab", None, None),
        P(None, "sub", "slab", None, None),
        P(),
        P(),
        P(),
        P(),
        P(),
        P(),
        P(),
        P(),
    )
    out_specs = (P("sub", "slab", None, None), P("sub", "slab", None), P("sub", "slab", None))
    return jax.shard_map(
        on_device, mesh=mesh, in_specs=in_specs, out_specs=out_specs, check_vma=False
    )
```

```python
import functools

import jax
import jax.numpy as jnp
from jax import lax
from jax.experimental import pallas as pl
from jax.experimental.pallas import tpu as pltpu
from jax.sharding import PartitionSpec as P

HI = lax.Precision.HIGHEST
F32 = jnp.float32
BF16 = jnp.bfloat16
VMEM_LIMIT = 60 * 1024 * 1024
N = 256
ROWS = 16
SLABS = 16
LANES = 128
GROUP = 4
FIELD = (SLABS, 2, N // SLABS, ROWS, LANES)


def params():
    return pltpu.CompilerParams(vmem_limit_bytes=VMEM_LIMIT)


def split(a):
    high = a.astype(BF16)
    low = (a - high.astype(F32)).astype(BF16)
    return high, low


def dot(a, b):
    return jnp.dot(a, b, preferred_element_type=F32)


def dot3(a, b):
    return dot(a[0], b[0]) + (dot(a[0], b[1]) + dot(a[1], b[0]))


def put_split(scratch, a):
    scratch[0], scratch[1] = split(a)


def whole(shape):
    return pl.BlockSpec(shape, lambda *_: (0,) * len(shape))


def smem():
    return pl.BlockSpec(memory_space=pltpu.SMEM)


def forward_kernel(source, coarse, basis_y, basis_z, out, left, right):
    step = pl.program_id(0)

    @pl.when(step == 0)
    def _():
        put_split(left, basis_y[...].T)
        put_split(right, basis_z[...])

    load = (source[...] + coarse[0, 0]).reshape(GROUP * N, N)
    first = dot3(split(load), right)
    for x in range(GROUP):
        part = dot3(left, split(first[x * N : x * N + N]))
        at = pl.ds((step * GROUP + x) % 8, ROWS, stride=8)
        for slab in range(SLABS):
            for half in range(2):
                rows = out.at[slab, half].reshape(ROWS * 8, LANES)
                piece = part[slab * ROWS : slab * ROWS + ROWS, LANES * half : LANES * half + LANES]
                rows[at, :] = piece


def forward(source, coarse, step, basis_y, basis_z):
    return pl.pallas_call(
        forward_kernel,
        grid=(ROWS // GROUP,),
        in_specs=[
            pl.BlockSpec((GROUP, N, N), lambda x: (x, 0, 0)),
            pl.BlockSpec((1, 1, GROUP, N, N), lambda x: (step, 0, x, 0, 0)),
            whole((N, N)),
            whole((N, N)),
        ],
        out_specs=pl.BlockSpec(
            (SLABS, 2, ROWS, 8, LANES), lambda x: (0, 0, 0, x * GROUP // 8, 0)
        ),
        out_shape=jax.ShapeDtypeStruct(FIELD, F32),
        scratch_shapes=[pltpu.VMEM((2, N, N), BF16), pltpu.VMEM((2, N, N), BF16)],
        compiler_params=params(),
        cost_estimate=pl.CostEstimate(
            flops=12 * ROWS * N**3, bytes_accessed=12 * ROWS * N * N, transcendentals=0
        ),
        name="forward",
    )(source, coarse, basis_y, basis_z)


def middle_kernel(base, shift, basis_x, lines, out, left, right):
    step = pl.program_id(0)

    @pl.when(step == 0)
    def _():
        put_split(left, basis_x[...].T)
        put_split(right, basis_x[...])

    for j in range(GROUP):
        halves = [lines[:, half, j].reshape(N, LANES) for half in range(2)]
        field = jnp.concatenate(halves, axis=1)
        modes = dot3(left, split(field)) / (base[...] + shift[step * GROUP + j])
        spread = dot3(right, split(modes))
        for half in range(2):
            piece = spread[:, LANES * half : LANES * half + LANES]
            out[:, half, j] = piece.reshape(SLABS, ROWS, LANES)


def middle(base, shift, basis_x, lines):
    block = pl.BlockSpec((SLABS, 2, GROUP, ROWS, LANES), lambda j: (0, 0, j, 0, 0))
    return pl.pallas_call(
        middle_kernel,
        grid=(N // SLABS // GROUP,),
        in_specs=[whole((N, N)), smem(), whole((N, N)), block],
        out_specs=block,
        out_shape=jax.ShapeDtypeStruct(FIELD, F32),
        scratch_shapes=[pltpu.VMEM((2, N, N), BF16), pltpu.VMEM((2, N, N), BF16)],
        compiler_params=params(),
        cost_estimate=pl.CostEstimate(
            flops=12 * ROWS * N**3, bytes_accessed=8 * ROWS * N * N, transcendentals=0
        ),
        name="middle",
    )(base, shift, basis_x, lines)


def backward_kernel(field, extra, basis_y, basis_z, out, left, right):
    step = pl.program_id(0)

    @pl.when(step == 0)
    def _():
        put_split(left, basis_y[...])
        put_split(right, basis_z[...].T)

    def total(x, slab, half):
        at = pl.ds((step * GROUP + x) % 8, ROWS, stride=8)
        terms = [ref.at[slab, half].reshape(ROWS * 8, LANES)[at, :] for ref in (field, extra)]
        return terms[0] + terms[1]

    parts = []
    for x in range(GROUP):
        halves = [
            jnp.concatenate([total(x, slab, half) for slab in range(SLABS)], axis=0)
            for half in range(2)
        ]
        parts.append(dot3(left, split(jnp.concatenate(halves, axis=1))))
    part = jnp.concatenate(parts, axis=0)
    out[...] = dot3(split(part), right).reshape(GROUP, N, N)


def backward(field, extra, basis_y, basis_z):
    block = pl.BlockSpec((SLABS, 2, ROWS, 8, LANES), lambda x: (0, 0, 0, x * GROUP // 8, 0))
    return pl.pallas_call(
        backward_kernel,
        grid=(ROWS // GROUP,),
        in_specs=[block, block, whole((N, N)), whole((N, N))],
        out_specs=pl.BlockSpec((GROUP, N, N), lambda x: (x, 0, 0)),
        out_shape=jax.ShapeDtypeStruct((ROWS, N, N), F32),
        scratch_shapes=[pltpu.VMEM((2, N, N), BF16), pltpu.VMEM((2, N, N), BF16)],
        compiler_params=params(),
        cost_estimate=pl.CostEstimate(
            flops=12 * ROWS * N**3, bytes_accessed=12 * ROWS * N * N, transcendentals=0
        ),
        name="backward",
    )(field, extra, basis_y, basis_z)


def inverse_parts(denom):
    high = pl.reciprocal(denom, approx=True).astype(BF16)
    wide = high.astype(F32)
    low = (wide * (1.0 - denom * wide)).astype(BF16)
    return high, low


def times_inverse(rows, denom):
    high, low = split(rows)
    count = rows.shape[0]
    w_high, w_low = inverse_parts(denom)
    both = dot(jnp.concatenate([high, low], axis=0), w_high)
    return both[:count] + (both[count:] + dot(high, w_low))


def faces_kernel(base, shift, own_x, ends, products, part0, part1, out):
    block = pl.program_id(0)
    first, last = ends[0:1], ends[1:2]
    for jj in range(ROWS):
        a = jnp.concatenate([part0[0, 0, jj], part0[0, 1, jj]], axis=1)
        b = jnp.concatenate([part1[0, 0, jj], part1[0, 1, jj]], axis=1)
        rows = jnp.concatenate([a * last, b * last, a * first, b * first, products[...]], axis=0)
        result = dot3(split(rows), inverse_parts(base[...] + shift[block * ROWS + jj]))
        for face in range(4):
            piece = result[16 * face : 16 * face + 16] * own_x[...]
            out[0, face, jj : jj + 1] = jnp.sum(piece, axis=0, keepdims=True)
        for pair in range(3):
            out[0, 4 + pair, jj : jj + 1] = result[64 + pair : 65 + pair]


def faces(base, shift, own_x, ends, products, part0, part1):
    block = pl.BlockSpec((1, 2, ROWS, ROWS, LANES), lambda j: (j, 0, 0, 0, 0))
    return pl.pallas_call(
        faces_kernel,
        grid=(N // ROWS,),
        in_specs=[
            whole((N, N)),
            smem(),
            whole((ROWS, N)),
            whole((2, N)),
            whole((16, N)),
            block,
            block,
        ],
        out_specs=pl.BlockSpec((1, 7, ROWS, N), lambda j: (j, 0, 0, 0)),
        out_shape=jax.ShapeDtypeStruct((SLABS, 7, N // SLABS, N), F32),
        compiler_params=params(),
        cost_estimate=pl.CostEstimate(
            flops=N**3, bytes_accessed=N * N, transcendentals=0
        ),
        name="faces",
    )(base, shift, own_x, ends, products, part0, part1)


def extra_kernel(base, shift, scale, own_x, ends, own, before, out):
    block = pl.program_id(0)
    alpha = scale[0]
    first, last = ends[0:1], ends[1:2]
    for jj in range(ROWS):
        upper = own_x[...] * (alpha * own[jj : jj + 1])
        lower = own_x[...] * (alpha * before[jj : jj + 1])
        rows = jnp.concatenate([upper, lower], axis=0)
        result = times_inverse(rows, base[...] + shift[block * ROWS + jj])
        result = first * result[16:] - last * result[:16]
        for half in range(2):
            out[0, half, jj] = result[:, LANES * half : LANES * half + LANES]


def extra(base, shift, scale, own_x, ends, own, before):
    return pl.pallas_call(
        extra_kernel,
        grid=(N // ROWS,),
        in_specs=[
            whole((N, N)),
            smem(),
            smem(),
            whole((ROWS, N)),
            whole((2, N)),
            pl.BlockSpec((ROWS, N), lambda j: (j, 0)),
            pl.BlockSpec((ROWS, N), lambda j: (j, 0)),
        ],
        out_specs=pl.BlockSpec((1, 2, ROWS, ROWS, LANES), lambda j: (j, 0, 0, 0, 0)),
        out_shape=jax.ShapeDtypeStruct(FIELD, F32),
        compiler_params=params(),
        cost_estimate=pl.CostEstimate(
            flops=N**3, bytes_accessed=N * N, transcendentals=0
        ),
        name="extra",
    )(base, shift, scale, own_x, ends, own, before)


def exact(a, b):
    return jnp.dot(a, b, precision=HI, preferred_element_type=F32)


def exact_t(a, b):
    dims = (((1,), (1,)), ((), ()))
    return lax.dot_general(a, b, dims, precision=HI, preferred_element_type=F32)


def precondition(jump, gram_x, gram_y, stiff):
    seen = exact(exact(gram_y, jump), gram_x)
    search = stiff * seen
    image = exact(exact(gram_y, search), gram_x)
    return search, image, jnp.sum(seen * search), jnp.sum(image * search)


def scalars_block(upper, lower):
    at = lax.broadcasted_iota(jnp.int32, (8, 128), 0)
    return jnp.where(at == 0, upper, jnp.where(at == 1, lower, 0.0))


def chain0_kernel(scale, jumps, gram_x, gram_y, stiff, search, image, sums):
    search[...], image[...], upper, lower = precondition(
        jumps[:, 0].reshape(N, N), gram_x[...], gram_y[...], scale[0] * stiff[...].T
    )
    sums[...] = scalars_block(upper, lower)


def chain0(*args):
    face = jax.ShapeDtypeStruct((N, N), F32)
    return pl.pallas_call(
        chain0_kernel,
        in_specs=[smem()] + [pl.BlockSpec(memory_space=pltpu.VMEM)] * 4,
        out_shape=(face, face, jax.ShapeDtypeStruct((8, 128), F32)),
        compiler_params=params(),
        cost_estimate=pl.CostEstimate(
            flops=N**3, bytes_accessed=N * N, transcendentals=0
        ),
        name="chain0",
    )(*args)


def chain1_kernel(
    scale, jumps, image, before, after, pieces, gram_x, gram_y, stiff, own_x, basis_y, search, sums, out
):
    alpha, ratio, weight = scale[0], scale[1], scale[2]
    t = image[...]
    table = [pieces[:, 4 + pair].reshape(N, N) for pair in range(3)]
    own = table[1] * before[...] - table[0] * t
    other = table[2] * t - table[1] * after[...]
    q = jumps[:, 1].reshape(N, N) + alpha * (own - ratio * other)
    search[...], _, upper, lower = precondition(
        q, gram_x[...], gram_y[...], weight * stiff[...].T
    )
    sums[...] = scalars_block(upper, lower)
    out[...] = exact_t(exact_t(own_x[...], q), basis_y[...])


def chain1(*args):
    return pl.pallas_call(
        chain1_kernel,
        in_specs=[smem()] + [pl.BlockSpec(memory_space=pltpu.VMEM)] * 10,
        out_shape=(
            jax.ShapeDtypeStruct((N, N), F32),
            jax.ShapeDtypeStruct((8, 128), F32),
            jax.ShapeDtypeStruct((ROWS, N), F32),
        ),
        compiler_params=params(),
        cost_estimate=pl.CostEstimate(
            flops=N**3, bytes_accessed=N * N, transcendentals=0
        ),
        name="chain1",
    )(*args)


def final_kernel(scale, search0, search1, own_x, basis_y, out):
    total = scale[0] * search0[...] + scale[1] * search1[...]
    out[...] = exact_t(exact_t(own_x[...], total), basis_y[...])


def final(*args):
    return pl.pallas_call(
        final_kernel,
        in_specs=[smem()] + [pl.BlockSpec(memory_space=pltpu.VMEM)] * 4,
        out_shape=jax.ShapeDtypeStruct((ROWS, N), F32),
        compiler_params=params(),
        cost_estimate=pl.CostEstimate(flops=N**3, bytes_accessed=N * N, transcendentals=0),
        name="final",
    )(*args)


def gram_kernel(basis_x, basis_y, gram_x, gram_y):
    gram_x[...] = exact(basis_x[...].T, basis_x[...])
    gram_y[...] = exact(basis_y[...].T, basis_y[...])


def grams(basis_x, basis_y):
    face = jax.ShapeDtypeStruct((N, N), F32)
    return pl.pallas_call(
        gram_kernel, out_shape=(face, face), compiler_params=params(), name="grams"
    )(basis_x, basis_y)


def from_behind(block, axis, distance):
    count = lax.axis_size(axis)
    route = [((i - distance) % count, i) for i in range(count)]
    return lax.ppermute(block, axis, route)


def sum_over_subs(sums):
    for bit in (1, 2, 4):
        sums = sums + lax.ppermute(sums, "sub", [(i, i ^ bit) for i in range(8)])
    return sums


def step_length(sums):
    return sums[0, 0] / (sums[1, 0] + 1e-06)


def exchange(block):
    return lax.all_to_all(block, "slab", split_axis=0, concat_axis=0, tiled=True)


def on_device(
    source, coarse, rho, basis_x, basis_y, basis_z, eigen_x, eigen_y, eigen_z, face_stiff
):
    source = source[0]
    sub_index = lax.axis_index("sub")
    slab_index = lax.axis_index("slab")
    subs = lax.axis_size("sub")
    own_rho = lax.dynamic_slice_in_dim(rho, sub_index, 1, 0)[0]
    next_rho = lax.dynamic_slice_in_dim(rho, (sub_index + 1) % subs, 1, 0)[0]
    weight = 0.5 * (own_rho + next_rho)
    start = slab_index * ROWS
    own_x = lax.dynamic_slice_in_dim(basis_x, start, ROWS, 0)

    part1 = forward(source, coarse, 1, basis_y, basis_z)
    lines = exchange(part1)

    base_xz = own_rho * (eigen_x[:, None] + eigen_z[None, :])
    base_zx = own_rho * (eigen_z[:, None] + eigen_x[None, :])
    shift = own_rho * eigen_y
    own_shift = lax.dynamic_slice_in_dim(shift, start, ROWS, 0)
    ends = jnp.stack([basis_z[0], basis_z[N - 1]])
    products = jnp.stack([ends[1] * ends[1], ends[1] * ends[0], ends[0] * ends[0]])
    products = jnp.pad(products, ((0, 13), (0, 0)))
    gram_x, gram_y = grams(basis_x, basis_y)

    part0 = forward(source, coarse, 0, basis_y, basis_z)
    pieces = faces(base_zx, shift, own_x, ends, products, part0, part1)
    following = from_behind(pieces[:, 2:4], "sub", -1)
    pieces, following, lines = lax.optimization_barrier((pieces, following, lines))
    shares = exchange(pieces[:, 0:2] - following)
    own_jumps = jnp.sum(shares, axis=0)
    jumps = exchange(jnp.broadcast_to(own_jumps[None], (SLABS,) + own_jumps.shape))

    spread = middle(base_xz, own_shift, basis_x, lines)
    spread, jumps = lax.optimization_barrier((spread, jumps))
    spread = exchange(spread)

    search0, image0, sums0 = chain0(weight.reshape(1), jumps, gram_x, gram_y, face_stiff)
    before = from_behind(image0, "sub", 1)
    after = from_behind(image0, "sub", -1)
    alpha0 = step_length(sum_over_subs(sums0))

    scale = jnp.stack([alpha0, own_rho / next_rho, weight])
    more = extra(base_xz, shift, scale, own_x, ends, image0, before)
    search1, sums1, jump = chain1(
        scale, jumps, image0, before, after, pieces, gram_x, gram_y, face_stiff, own_x, basis_y
    )
    alpha1 = step_length(sum_over_subs(sums1))
    multipliers = final(jnp.stack([alpha0, alpha1]), search0, search1, own_x, basis_y)
    solution = backward(spread, more, basis_y, basis_z)
    return (solution[None], multipliers[None], jump[None])


def solution(mesh):
    in_specs = (
        P("sub", "slab", None, None),
        P(None, "sub", "slab", None, None),
        P(),
        P(),
        P(),
        P(),
        P(),
        P(),
        P(),
        P(),
    )
    out_specs = (P("sub", "slab", None, None), P("sub", "slab", None), P("sub", "slab", None))
    return jax.shard_map(
        on_device, mesh=mesh, in_specs=in_specs, out_specs=out_specs, check_vma=False
    )
```

```python
import functools

import jax
import jax.numpy as jnp
from jax import lax
from jax.experimental import pallas as pl
from jax.experimental.pallas import tpu as pltpu
from jax.sharding import PartitionSpec as P

HI = lax.Precision.HIGHEST
F32 = jnp.float32
BF16 = jnp.bfloat16
VMEM_LIMIT = 60 * 1024 * 1024
N = 256
ROWS = 16
SLABS = 16
LANES = 128
GROUP = 8
PARTS = 4
EXTRA_COST = 6 * 10**9
FIELD = (SLABS, 2, N // SLABS, ROWS, LANES)


def params():
    return pltpu.CompilerParams(vmem_limit_bytes=VMEM_LIMIT)


def split(a):
    high = a.astype(BF16)
    low = (a - high.astype(F32)).astype(BF16)
    return high, low


def dot(a, b):
    return jnp.dot(a, b, preferred_element_type=F32)


def dot3(a, b):
    return dot(a[0], b[0]) + (dot(a[0], b[1]) + dot(a[1], b[0]))


def put_split(scratch, a):
    scratch[0], scratch[1] = split(a)


def whole(shape):
    return pl.BlockSpec(shape, lambda *_: (0,) * len(shape))


def smem():
    return pl.BlockSpec(memory_space=pltpu.SMEM)


def forward_kernel(source, coarse, basis_y, basis_z, out, left, right):
    step = pl.program_id(0)

    @pl.when(step == 0)
    def _():
        put_split(left, basis_y[...].T)
        put_split(right, basis_z[...])

    load = (source[...] + coarse[0, 0]).reshape(GROUP * N, N)
    first = dot3(split(load), right)
    for x in range(GROUP):
        part = dot3(left, split(first[x * N : x * N + N]))
        at = pl.ds((step * GROUP + x) % 8, ROWS, stride=8)
        for slab in range(SLABS):
            for half in range(2):
                rows = out.at[slab, half].reshape(ROWS * 8, LANES)
                piece = part[slab * ROWS : slab * ROWS + ROWS, LANES * half : LANES * half + LANES]
                rows[at, :] = piece


def forward(source, coarse, step, basis_y, basis_z):
    return pl.pallas_call(
        forward_kernel,
        grid=(ROWS // GROUP,),
        in_specs=[
            pl.BlockSpec((GROUP, N, N), lambda x: (x, 0, 0)),
            pl.BlockSpec((1, 1, GROUP, N, N), lambda x: (step, 0, x, 0, 0)),
            whole((N, N)),
            whole((N, N)),
        ],
        out_specs=pl.BlockSpec(
            (SLABS, 2, ROWS, 8, LANES), lambda x: (0, 0, 0, x * GROUP // 8, 0)
        ),
        out_shape=jax.ShapeDtypeStruct(FIELD, F32),
        scratch_shapes=[pltpu.VMEM((2, N, N), BF16), pltpu.VMEM((2, N, N), BF16)],
        compiler_params=params(),
        cost_estimate=pl.CostEstimate(
            flops=12 * ROWS * N**3, bytes_accessed=12 * ROWS * N * N, transcendentals=0
        ),
        name="forward",
    )(source, coarse, basis_y, basis_z)


def middle_kernel(base, shift, basis_x, lines, out, left, right):
    step = pl.program_id(0)

    @pl.when(step == 0)
    def _():
        put_split(left, basis_x[...].T)
        put_split(right, basis_x[...])

    for j in range(GROUP):
        halves = [lines[:, half, j].reshape(N, LANES) for half in range(2)]
        field = jnp.concatenate(halves, axis=1)
        modes = dot3(left, split(field)) / (base[...] + shift[step * GROUP + j])
        spread = dot3(right, split(modes))
        for half in range(2):
            piece = spread[:, LANES * half : LANES * half + LANES]
            out[:, half, j] = piece.reshape(SLABS, ROWS, LANES)


def middle(base, shift, basis_x, lines):
    block = pl.BlockSpec((SLABS, 2, GROUP, ROWS, LANES), lambda j: (0, 0, j, 0, 0))
    return pl.pallas_call(
        middle_kernel,
        grid=(N // SLABS // GROUP,),
        in_specs=[whole((N, N)), smem(), whole((N, N)), block],
        out_specs=block,
        out_shape=jax.ShapeDtypeStruct(FIELD, F32),
        scratch_shapes=[pltpu.VMEM((2, N, N), BF16), pltpu.VMEM((2, N, N), BF16)],
        compiler_params=params(),
        cost_estimate=pl.CostEstimate(
            flops=12 * ROWS * N**3, bytes_accessed=8 * ROWS * N * N, transcendentals=0
        ),
        name="middle",
    )(base, shift, basis_x, lines)


def backward_kernel(scale, field, extra, basis_y, basis_z, out, left, right):
    step = pl.program_id(0)

    @pl.when(step == 0)
    def _():
        put_split(left, basis_y[...])
        put_split(right, basis_z[...].T)

    def total(x, slab, half):
        at = pl.ds((step * GROUP + x) % 8, ROWS, stride=8)
        terms = [ref.at[slab, half].reshape(ROWS * 8, LANES)[at, :] for ref in (field, extra)]
        return terms[0] + scale[0] * terms[1]

    parts = []
    for x in range(GROUP):
        halves = [
            jnp.concatenate([total(x, slab, half) for slab in range(SLABS)], axis=0)
            for half in range(2)
        ]
        parts.append(dot3(left, split(jnp.concatenate(halves, axis=1))))
    part = jnp.concatenate(parts, axis=0)
    out[...] = dot3(split(part), right).reshape(GROUP, N, N)


def backward(scale, field, extra, basis_y, basis_z):
    block = pl.BlockSpec((SLABS, 2, ROWS, 8, LANES), lambda x: (0, 0, 0, x * GROUP // 8, 0))
    return pl.pallas_call(
        backward_kernel,
        grid=(ROWS // GROUP,),
        in_specs=[smem(), block, block, whole((N, N)), whole((N, N))],
        out_specs=pl.BlockSpec((GROUP, N, N), lambda x: (x, 0, 0)),
        out_shape=jax.ShapeDtypeStruct((ROWS, N, N), F32),
        scratch_shapes=[pltpu.VMEM((2, N, N), BF16), pltpu.VMEM((2, N, N), BF16)],
        compiler_params=params(),
        cost_estimate=pl.CostEstimate(
            flops=12 * ROWS * N**3, bytes_accessed=12 * ROWS * N * N, transcendentals=0
        ),
        name="backward",
    )(scale, field, extra, basis_y, basis_z)


def inverse_parts(denom):
    high = pl.reciprocal(denom, approx=True).astype(BF16)
    wide = high.astype(F32)
    low = (wide * (1.0 - denom * wide)).astype(BF16)
    return high, low


def times_inverse(rows, denom):
    high, low = split(rows)
    count = rows.shape[0]
    w_high, w_low = inverse_parts(denom)
    both = dot(jnp.concatenate([high, low], axis=0), w_high)
    return both[:count] + (both[count:] + dot(high, w_low))


def faces_kernel(base, shift, own_x, ends, products, part0, part1, out):
    block = pl.program_id(0)
    first, last = ends[0:1], ends[1:2]
    for jj in range(ROWS):
        a = jnp.concatenate([part0[0, 0, jj], part0[0, 1, jj]], axis=1)
        b = jnp.concatenate([part1[0, 0, jj], part1[0, 1, jj]], axis=1)
        rows = jnp.concatenate([a * last, b * last, a * first, b * first, products[...]], axis=0)
        result = dot3(split(rows), inverse_parts(base[...] + shift[block * ROWS + jj]))
        for face in range(4):
            piece = result[16 * face : 16 * face + 16] * own_x[...]
            out[0, face, jj : jj + 1] = jnp.sum(piece, axis=0, keepdims=True)
        for pair in range(3):
            out[0, 4 + pair, jj : jj + 1] = result[64 + pair : 65 + pair]


def faces(base, shift, own_x, ends, products, part0, part1):
    block = pl.BlockSpec((1, 2, ROWS, ROWS, LANES), lambda j: (j, 0, 0, 0, 0))
    return pl.pallas_call(
        faces_kernel,
        grid=(N // ROWS,),
        in_specs=[
            whole((N, N)),
            smem(),
            whole((ROWS, N)),
            whole((2, N)),
            whole((16, N)),
            block,
            block,
        ],
        out_specs=pl.BlockSpec((1, 7, ROWS, N), lambda j: (j, 0, 0, 0)),
        out_shape=jax.ShapeDtypeStruct((SLABS, 7, N // SLABS, N), F32),
        compiler_params=params(),
        cost_estimate=pl.CostEstimate(
            flops=N**3, bytes_accessed=N * N, transcendentals=0
        ),
        name="faces",
    )(base, shift, own_x, ends, products, part0, part1)


def extra_kernel(part, base, shift, own_x, ends, own, before, *refs):
    out = refs[-1]
    block = part * (SLABS // PARTS) + pl.program_id(0)
    first, last = ends[0:1], ends[1:2]
    for jj in range(ROWS):
        upper = own_x[...] * own[jj : jj + 1]
        lower = own_x[...] * before[jj : jj + 1]
        rows = jnp.concatenate([upper, lower], axis=0)
        result = times_inverse(rows, base[...] + shift[block * ROWS + jj])
        result = first * result[16:] - last * result[:16]
        for half in range(2):
            out[0, half, jj] = result[:, LANES * half : LANES * half + LANES]


def extra(part, base, shift, own_x, ends, own, before, filled=()):
    skip = part * (SLABS // PARTS)
    return pl.pallas_call(
        functools.partial(extra_kernel, part),
        grid=(SLABS // PARTS,),
        in_specs=[
            whole((N, N)),
            smem(),
            whole((ROWS, N)),
            whole((2, N)),
            pl.BlockSpec((ROWS, N), lambda j: (skip + j, 0)),
            pl.BlockSpec((ROWS, N), lambda j: (skip + j, 0)),
        ]
        + [pl.BlockSpec(memory_space=pl.ANY)] * len(filled),
        out_specs=pl.BlockSpec((1, 2, ROWS, ROWS, LANES), lambda j: (skip + j, 0, 0, 0, 0)),
        out_shape=jax.ShapeDtypeStruct(FIELD, F32),
        input_output_aliases={6: 0} if filled else {},
        compiler_params=params(),
        cost_estimate=pl.CostEstimate(
            flops=EXTRA_COST, bytes_accessed=4 * ROWS * N * N // PARTS, transcendentals=0
        ),
        name=f"extra{part}",
    )(base, shift, own_x, ends, own, before, *filled)


def exact(a, b):
    return jnp.dot(a, b, precision=HI, preferred_element_type=F32)


def exact_t(a, b):
    dims = (((1,), (1,)), ((), ()))
    return lax.dot_general(a, b, dims, precision=HI, preferred_element_type=F32)


def precondition(jump, gram_x, gram_y, stiff):
    seen = exact(exact(gram_y, jump), gram_x)
    search = stiff * seen
    image = exact(exact(gram_y, search), gram_x)
    return search, image, jnp.sum(seen * search), jnp.sum(image * search)


def scalars_block(upper, lower):
    at = lax.broadcasted_iota(jnp.int32, (8, 128), 0)
    return jnp.where(at == 0, upper, jnp.where(at == 1, lower, 0.0))


def chain0_kernel(scale, jumps, gram_x, gram_y, stiff, search, image, sums):
    search[...], image[...], upper, lower = precondition(
        jumps[:, 0].reshape(N, N), gram_x[...], gram_y[...], scale[0] * stiff[...].T
    )
    sums[...] = scalars_block(upper, lower)


def chain0(*args):
    face = jax.ShapeDtypeStruct((N, N), F32)
    return pl.pallas_call(
        chain0_kernel,
        in_specs=[smem()] + [pl.BlockSpec(memory_space=pltpu.VMEM)] * 4,
        out_shape=(face, face, jax.ShapeDtypeStruct((8, 128), F32)),
        compiler_params=params(),
        cost_estimate=pl.CostEstimate(
            flops=N**3, bytes_accessed=N * N, transcendentals=0
        ),
        name="chain0",
    )(*args)


def chain1_kernel(
    scale, jumps, image, before, after, pieces, gram_x, gram_y, stiff, own_x, basis_y, search, sums, out
):
    alpha, ratio, weight = scale[0], scale[1], scale[2]
    t = image[...]
    table = [pieces[:, 4 + pair].reshape(N, N) for pair in range(3)]
    own = table[1] * before[...] - table[0] * t
    other = table[2] * t - table[1] * after[...]
    q = jumps[:, 1].reshape(N, N) + alpha * (own - ratio * other)
    search[...], _, upper, lower = precondition(
        q, gram_x[...], gram_y[...], weight * stiff[...].T
    )
    sums[...] = scalars_block(upper, lower)
    out[...] = exact_t(exact_t(own_x[...], q), basis_y[...])


def chain1(*args):
    return pl.pallas_call(
        chain1_kernel,
        in_specs=[smem()] + [pl.BlockSpec(memory_space=pltpu.VMEM)] * 10,
        out_shape=(
            jax.ShapeDtypeStruct((N, N), F32),
            jax.ShapeDtypeStruct((8, 128), F32),
            jax.ShapeDtypeStruct((ROWS, N), F32),
        ),
        compiler_params=params(),
        cost_estimate=pl.CostEstimate(
            flops=N**3, bytes_accessed=N * N, transcendentals=0
        ),
        name="chain1",
    )(*args)


def final_kernel(scale, search0, search1, own_x, basis_y, out):
    total = scale[0] * search0[...] + scale[1] * search1[...]
    out[...] = exact_t(exact_t(own_x[...], total), basis_y[...])


def final(*args):
    return pl.pallas_call(
        final_kernel,
        in_specs=[smem()] + [pl.BlockSpec(memory_space=pltpu.VMEM)] * 4,
        out_shape=jax.ShapeDtypeStruct((ROWS, N), F32),
        compiler_params=params(),
        cost_estimate=pl.CostEstimate(flops=N**3, bytes_accessed=N * N, transcendentals=0),
        name="final",
    )(*args)


def gram_kernel(basis_x, basis_y, gram_x, gram_y):
    gram_x[...] = exact(basis_x[...].T, basis_x[...])
    gram_y[...] = exact(basis_y[...].T, basis_y[...])


def grams(basis_x, basis_y):
    face = jax.ShapeDtypeStruct((N, N), F32)
    return pl.pallas_call(
        gram_kernel, out_shape=(face, face), compiler_params=params(), name="grams"
    )(basis_x, basis_y)


def from_behind(block, axis, distance):
    count = lax.axis_size(axis)
    route = [((i - distance) % count, i) for i in range(count)]
    return lax.ppermute(block, axis, route)


def with_partner(sums, bit):
    return sums + lax.ppermute(sums, "sub", [(i, i ^ bit) for i in range(8)])


def step_length(sums):
    return sums[0, 0] / (sums[1, 0] + 1e-06)


def exchange(block):
    return lax.all_to_all(block, "slab", split_axis=0, concat_axis=0, tiled=True)


def on_device(
    source, coarse, rho, basis_x, basis_y, basis_z, eigen_x, eigen_y, eigen_z, face_stiff
):
    source = source[0]
    sub_index = lax.axis_index("sub")
    slab_index = lax.axis_index("slab")
    subs = lax.axis_size("sub")
    own_rho = lax.dynamic_slice_in_dim(rho, sub_index, 1, 0)[0]
    next_rho = lax.dynamic_slice_in_dim(rho, (sub_index + 1) % subs, 1, 0)[0]
    weight = 0.5 * (own_rho + next_rho)
    start = slab_index * ROWS
    own_x = lax.dynamic_slice_in_dim(basis_x, start, ROWS, 0)

    part1 = forward(source, coarse, 1, basis_y, basis_z)
    lines = exchange(part1)

    base_xz = own_rho * (eigen_x[:, None] + eigen_z[None, :])
    base_zx = own_rho * (eigen_z[:, None] + eigen_x[None, :])
    shift = own_rho * eigen_y
    own_shift = lax.dynamic_slice_in_dim(shift, start, ROWS, 0)
    ends = jnp.stack([basis_z[0], basis_z[N - 1]])
    products = jnp.stack([ends[1] * ends[1], ends[1] * ends[0], ends[0] * ends[0]])
    products = jnp.pad(products, ((0, 13), (0, 0)))
    gram_x, gram_y = grams(basis_x, basis_y)

    part0 = forward(source, coarse, 0, basis_y, basis_z)
    pieces = faces(base_zx, shift, own_x, ends, products, part0, part1)
    following = from_behind(pieces[:, 2:4], "sub", -1)
    pieces, following, lines, gram_x, gram_y = lax.optimization_barrier(
        (pieces, following, lines, gram_x, gram_y)
    )
    spread = middle(base_xz, own_shift, basis_x, lines)
    shares = exchange(pieces[:, 0:2] - following)
    shares, spread = lax.optimization_barrier((shares, spread))
    own_jumps = jnp.sum(shares, axis=0)
    jumps = exchange(jnp.broadcast_to(own_jumps[None], (SLABS,) + own_jumps.shape))

    spread, jumps = lax.optimization_barrier((spread, jumps))
    spread = exchange(spread)

    search0, image0, sums0 = chain0(weight.reshape(1), jumps, gram_x, gram_y, face_stiff)
    before = from_behind(image0, "sub", 1)
    after = from_behind(image0, "sub", -1)

    terms = functools.partial(extra, base=base_xz, shift=shift, own_x=own_x, ends=ends)
    more = terms(0, own=image0, before=before)
    sums0, more = lax.optimization_barrier((with_partner(sums0, 1), more))
    more = terms(1, own=image0, before=before, filled=(more,))
    sums0, more = lax.optimization_barrier((with_partner(sums0, 2), more))
    alpha0 = step_length(with_partner(sums0, 4))

    scale = jnp.stack([alpha0, own_rho / next_rho, weight])
    search1, sums1, jump = chain1(
        scale, jumps, image0, before, after, pieces, gram_x, gram_y, face_stiff, own_x, basis_y
    )
    sums1, more = lax.optimization_barrier((sums1, more))
    more = terms(2, own=image0, before=before, filled=(more,))
    sums1, more = lax.optimization_barrier((with_partner(sums1, 1), more))
    more = terms(3, own=image0, before=before, filled=(more,))
    sums1, more = lax.optimization_barrier((with_partner(sums1, 2), more))
    alpha1 = step_length(with_partner(sums1, 4))
    multipliers = final(jnp.stack([alpha0, alpha1]), search0, search1, own_x, basis_y)
    solution = backward(scale, spread, more, basis_y, basis_z)
    return (solution[None], multipliers[None], jump[None])


def solution(mesh):
    in_specs = (
        P("sub", "slab", None, None),
        P(None, "sub", "slab", None, None),
        P(),
        P(),
        P(),
        P(),
        P(),
        P(),
        P(),
        P(),
    )
    out_specs = (P("sub", "slab", None, None), P("sub", "slab", None), P("sub", "slab", None))
    return jax.shard_map(
        on_device, mesh=mesh, in_specs=in_specs, out_specs=out_specs, check_vma=False
    )
```

```python
import functools

import jax
import jax.numpy as jnp
from jax import lax
from jax.experimental import pallas as pl
from jax.experimental.pallas import tpu as pltpu
from jax.sharding import PartitionSpec as P

HI = lax.Precision.HIGHEST
F32 = jnp.float32
BF16 = jnp.bfloat16
VMEM_LIMIT = 60 * 1024 * 1024
N = 256
ROWS = 16
SLABS = 16
LANES = 128
GROUP = 8
PARTS = ((0, 6), (6, 11), (11, 16))
BLOCK_COST = 15 * 10**8
FIELD = (SLABS, 2, N // SLABS, ROWS, LANES)


def params():
    return pltpu.CompilerParams(vmem_limit_bytes=VMEM_LIMIT)


def split(a):
    high = a.astype(BF16)
    low = (a - high.astype(F32)).astype(BF16)
    return high, low


def dot(a, b):
    return jnp.dot(a, b, preferred_element_type=F32)


def dot3(a, b):
    return dot(a[0], b[0]) + (dot(a[0], b[1]) + dot(a[1], b[0]))


def put_split(scratch, a):
    scratch[0], scratch[1] = split(a)


def whole(shape):
    return pl.BlockSpec(shape, lambda *_: (0,) * len(shape))


def smem():
    return pl.BlockSpec(memory_space=pltpu.SMEM)


def forward_kernel(source, coarse, basis_y, basis_z, out, left, right):
    step = pl.program_id(0)

    @pl.when(step == 0)
    def _():
        put_split(left, basis_y[...].T)
        put_split(right, basis_z[...])

    load = (source[...] + coarse[0, 0]).reshape(GROUP * N, N)
    first = dot3(split(load), right)
    for x in range(GROUP):
        part = dot3(left, split(first[x * N : x * N + N]))
        at = pl.ds((step * GROUP + x) % 8, ROWS, stride=8)
        for slab in range(SLABS):
            for half in range(2):
                rows = out.at[slab, half].reshape(ROWS * 8, LANES)
                piece = part[slab * ROWS : slab * ROWS + ROWS, LANES * half : LANES * half + LANES]
                rows[at, :] = piece


def forward(source, coarse, step, basis_y, basis_z):
    return pl.pallas_call(
        forward_kernel,
        grid=(ROWS // GROUP,),
        in_specs=[
            pl.BlockSpec((GROUP, N, N), lambda x: (x, 0, 0)),
            pl.BlockSpec((1, 1, GROUP, N, N), lambda x: (step, 0, x, 0, 0)),
            whole((N, N)),
            whole((N, N)),
        ],
        out_specs=pl.BlockSpec(
            (SLABS, 2, ROWS, 8, LANES), lambda x: (0, 0, 0, x * GROUP // 8, 0)
        ),
        out_shape=jax.ShapeDtypeStruct(FIELD, F32),
        scratch_shapes=[pltpu.VMEM((2, N, N), BF16), pltpu.VMEM((2, N, N), BF16)],
        compiler_params=params(),
        cost_estimate=pl.CostEstimate(
            flops=12 * ROWS * N**3, bytes_accessed=12 * ROWS * N * N, transcendentals=0
        ),
        name="forward",
    )(source, coarse, basis_y, basis_z)


def middle_kernel(base, shift, basis_x, lines, out, left, right):
    step = pl.program_id(0)

    @pl.when(step == 0)
    def _():
        put_split(left, basis_x[...].T)
        put_split(right, basis_x[...])

    for j in range(GROUP):
        halves = [lines[:, half, j].reshape(N, LANES) for half in range(2)]
        field = jnp.concatenate(halves, axis=1)
        modes = dot3(left, split(field)) / (base[...] + shift[step * GROUP + j])
        spread = dot3(right, split(modes))
        for half in range(2):
            piece = spread[:, LANES * half : LANES * half + LANES]
            out[:, half, j] = piece.reshape(SLABS, ROWS, LANES)


def middle(base, shift, basis_x, lines):
    block = pl.BlockSpec((SLABS, 2, GROUP, ROWS, LANES), lambda j: (0, 0, j, 0, 0))
    return pl.pallas_call(
        middle_kernel,
        grid=(N // SLABS // GROUP,),
        in_specs=[whole((N, N)), smem(), whole((N, N)), block],
        out_specs=block,
        out_shape=jax.ShapeDtypeStruct(FIELD, F32),
        scratch_shapes=[pltpu.VMEM((2, N, N), BF16), pltpu.VMEM((2, N, N), BF16)],
        compiler_params=params(),
        cost_estimate=pl.CostEstimate(
            flops=12 * ROWS * N**3, bytes_accessed=8 * ROWS * N * N, transcendentals=0
        ),
        name="middle",
    )(base, shift, basis_x, lines)


def backward_kernel(scale, field, extra, basis_y, basis_z, out, left, right):
    step = pl.program_id(0)

    @pl.when(step == 0)
    def _():
        put_split(left, basis_y[...])
        put_split(right, basis_z[...].T)

    def total(x, slab, half):
        at = pl.ds((step * GROUP + x) % 8, ROWS, stride=8)
        terms = [ref.at[slab, half].reshape(ROWS * 8, LANES)[at, :] for ref in (field, extra)]
        return terms[0] + scale[0] * terms[1]

    parts = []
    for x in range(GROUP):
        halves = [
            jnp.concatenate([total(x, slab, half) for slab in range(SLABS)], axis=0)
            for half in range(2)
        ]
        parts.append(dot3(left, split(jnp.concatenate(halves, axis=1))))
    part = jnp.concatenate(parts, axis=0)
    out[...] = dot3(split(part), right).reshape(GROUP, N, N)


def backward(scale, field, extra, basis_y, basis_z):
    block = pl.BlockSpec((SLABS, 2, ROWS, 8, LANES), lambda x: (0, 0, 0, x * GROUP // 8, 0))
    return pl.pallas_call(
        backward_kernel,
        grid=(ROWS // GROUP,),
        in_specs=[smem(), block, block, whole((N, N)), whole((N, N))],
        out_specs=pl.BlockSpec((GROUP, N, N), lambda x: (x, 0, 0)),
        out_shape=jax.ShapeDtypeStruct((ROWS, N, N), F32),
        scratch_shapes=[pltpu.VMEM((2, N, N), BF16), pltpu.VMEM((2, N, N), BF16)],
        compiler_params=params(),
        cost_estimate=pl.CostEstimate(
            flops=12 * ROWS * N**3, bytes_accessed=12 * ROWS * N * N, transcendentals=0
        ),
        name="backward",
    )(scale, field, extra, basis_y, basis_z)


def inverse_parts(denom):
    high = pl.reciprocal(denom, approx=True).astype(BF16)
    wide = high.astype(F32)
    low = (wide * (1.0 - denom * wide)).astype(BF16)
    return high, low


def times_inverse(rows, denom):
    high, low = split(rows)
    count = rows.shape[0]
    w_high, w_low = inverse_parts(denom)
    both = dot(jnp.concatenate([high, low], axis=0), w_high)
    return both[:count] + (both[count:] + dot(high, w_low))


def faces_kernel(base, shift, own_x, ends, products, part0, part1, out):
    block = pl.program_id(0)
    first, last = ends[0:1], ends[1:2]
    for jj in range(ROWS):
        a = jnp.concatenate([part0[0, 0, jj], part0[0, 1, jj]], axis=1)
        b = jnp.concatenate([part1[0, 0, jj], part1[0, 1, jj]], axis=1)
        rows = jnp.concatenate([a * last, b * last, a * first, b * first, products[...]], axis=0)
        result = dot3(split(rows), inverse_parts(base[...] + shift[block * ROWS + jj]))
        for face in range(4):
            piece = result[16 * face : 16 * face + 16] * own_x[...]
            out[0, face, jj : jj + 1] = jnp.sum(piece, axis=0, keepdims=True)
        for pair in range(3):
            out[0, 4 + pair, jj : jj + 1] = result[64 + pair : 65 + pair]


def faces(base, shift, own_x, ends, products, part0, part1):
    block = pl.BlockSpec((1, 2, ROWS, ROWS, LANES), lambda j: (j, 0, 0, 0, 0))
    return pl.pallas_call(
        faces_kernel,
        grid=(N // ROWS,),
        in_specs=[
            whole((N, N)),
            smem(),
            whole((ROWS, N)),
            whole((2, N)),
            whole((16, N)),
            block,
            block,
        ],
        out_specs=pl.BlockSpec((1, 7, ROWS, N), lambda j: (j, 0, 0, 0)),
        out_shape=jax.ShapeDtypeStruct((SLABS, 7, N // SLABS, N), F32),
        compiler_params=params(),
        cost_estimate=pl.CostEstimate(
            flops=N**3, bytes_accessed=N * N, transcendentals=0
        ),
        name="faces",
    )(base, shift, own_x, ends, products, part0, part1)


def extra_kernel(part, base, shift, own_x, ends, own, before, *refs):
    out = refs[-1]
    block = PARTS[part][0] + pl.program_id(0)
    first, last = ends[0:1], ends[1:2]
    for jj in range(ROWS):
        upper = own_x[...] * own[jj : jj + 1]
        lower = own_x[...] * before[jj : jj + 1]
        rows = jnp.concatenate([upper, lower], axis=0)
        result = times_inverse(rows, base[...] + shift[block * ROWS + jj])
        result = first * result[16:] - last * result[:16]
        for half in range(2):
            out[0, half, jj] = result[:, LANES * half : LANES * half + LANES]


def extra(part, base, shift, own_x, ends, own, before, filled=()):
    skip, stop = PARTS[part]
    return pl.pallas_call(
        functools.partial(extra_kernel, part),
        grid=(stop - skip,),
        in_specs=[
            whole((N, N)),
            smem(),
            whole((ROWS, N)),
            whole((2, N)),
            pl.BlockSpec((ROWS, N), lambda j: (skip + j, 0)),
            pl.BlockSpec((ROWS, N), lambda j: (skip + j, 0)),
        ]
        + [pl.BlockSpec(memory_space=pl.ANY)] * len(filled),
        out_specs=pl.BlockSpec((1, 2, ROWS, ROWS, LANES), lambda j: (skip + j, 0, 0, 0, 0)),
        out_shape=jax.ShapeDtypeStruct(FIELD, F32),
        input_output_aliases={6: 0} if filled else {},
        compiler_params=params(),
        cost_estimate=pl.CostEstimate(
            flops=BLOCK_COST * (stop - skip), bytes_accessed=N * N, transcendentals=0
        ),
        name=f"extra{part}",
    )(base, shift, own_x, ends, own, before, *filled)


def exact(a, b):
    return jnp.dot(a, b, precision=HI, preferred_element_type=F32)


def exact_t(a, b):
    dims = (((1,), (1,)), ((), ()))
    return lax.dot_general(a, b, dims, precision=HI, preferred_element_type=F32)


def precondition(jump, gram_x, gram_y, stiff):
    seen = exact(exact(gram_y, jump), gram_x)
    search = stiff * seen
    image = exact(exact(gram_y, search), gram_x)
    return search, image, jnp.sum(seen * search), jnp.sum(image * search)


def scalars_block(upper, lower):
    at = lax.broadcasted_iota(jnp.int32, (8, 128), 0)
    return jnp.where(at == 0, upper, jnp.where(at == 1, lower, 0.0))


def chain0_kernel(scale, jumps, gram_x, gram_y, stiff, own_x, basis_y, rows, image, sums):
    search, image[...], upper, lower = precondition(
        jumps[:, 0].reshape(N, N), gram_x[...], gram_y[...], scale[0] * stiff[...].T
    )
    sums[...] = scalars_block(upper, lower)
    rows[...] = exact_t(exact_t(own_x[...], search), basis_y[...])


def chain0(*args):
    face = jax.ShapeDtypeStruct((N, N), F32)
    return pl.pallas_call(
        chain0_kernel,
        in_specs=[smem()] + [pl.BlockSpec(memory_space=pltpu.VMEM)] * 6,
        out_shape=(jax.ShapeDtypeStruct((ROWS, N), F32), face, jax.ShapeDtypeStruct((8, 128), F32)),
        compiler_params=params(),
        cost_estimate=pl.CostEstimate(
            flops=N**3, bytes_accessed=N * N, transcendentals=0
        ),
        name="chain0",
    )(*args)


def chain1_kernel(
    scale, jumps, image, before, after, pieces, gram_x, gram_y, stiff, own_x, basis_y, sums, out, rows
):
    alpha, ratio, weight = scale[0], scale[1], scale[2]
    t = image[...]
    table = [pieces[:, 4 + pair].reshape(N, N) for pair in range(3)]
    own = table[1] * before[...] - table[0] * t
    other = table[2] * t - table[1] * after[...]
    q = jumps[:, 1].reshape(N, N) + alpha * (own - ratio * other)
    search, _, upper, lower = precondition(
        q, gram_x[...], gram_y[...], weight * stiff[...].T
    )
    sums[...] = scalars_block(upper, lower)
    out[...] = exact_t(exact_t(own_x[...], q), basis_y[...])
    rows[...] = exact_t(exact_t(own_x[...], search), basis_y[...])


def chain1(*args):
    return pl.pallas_call(
        chain1_kernel,
        in_specs=[smem()] + [pl.BlockSpec(memory_space=pltpu.VMEM)] * 10,
        out_shape=(
            jax.ShapeDtypeStruct((8, 128), F32),
            jax.ShapeDtypeStruct((ROWS, N), F32),
            jax.ShapeDtypeStruct((ROWS, N), F32),
        ),
        compiler_params=params(),
        cost_estimate=pl.CostEstimate(
            flops=N**3, bytes_accessed=N * N, transcendentals=0
        ),
        name="chain1",
    )(*args)


def gram_kernel(basis_x, basis_y, gram_x, gram_y):
    gram_x[...] = exact(basis_x[...].T, basis_x[...])
    gram_y[...] = exact(basis_y[...].T, basis_y[...])


def grams(basis_x, basis_y):
    face = jax.ShapeDtypeStruct((N, N), F32)
    return pl.pallas_call(
        gram_kernel, out_shape=(face, face), compiler_params=params(), name="grams"
    )(basis_x, basis_y)


def from_behind(block, axis, distance):
    count = lax.axis_size(axis)
    route = [((i - distance) % count, i) for i in range(count)]
    return lax.ppermute(block, axis, route)


def from_partner(sums, bits):
    return lax.ppermute(sums, "sub", [(i, i ^ bits) for i in range(8)])


def over_pair(sums):
    return sums + from_partner(sums, 1)


def over_pairs(sums):
    return (sums + from_partner(sums, 2)) + (from_partner(sums, 4) + from_partner(sums, 6))


def step_length(sums):
    return sums[0, 0] / (sums[1, 0] + 1e-06)


def exchange(block):
    return lax.all_to_all(block, "slab", split_axis=0, concat_axis=0, tiled=True)


def on_device(
    source, coarse, rho, basis_x, basis_y, basis_z, eigen_x, eigen_y, eigen_z, face_stiff
):
    source = source[0]
    sub_index = lax.axis_index("sub")
    slab_index = lax.axis_index("slab")
    subs = lax.axis_size("sub")
    own_rho = lax.dynamic_slice_in_dim(rho, sub_index, 1, 0)[0]
    next_rho = lax.dynamic_slice_in_dim(rho, (sub_index + 1) % subs, 1, 0)[0]
    weight = 0.5 * (own_rho + next_rho)
    start = slab_index * ROWS
    own_x = lax.dynamic_slice_in_dim(basis_x, start, ROWS, 0)

    part1 = forward(source, coarse, 1, basis_y, basis_z)
    lines = exchange(part1)

    base_xz = own_rho * (eigen_x[:, None] + eigen_z[None, :])
    base_zx = own_rho * (eigen_z[:, None] + eigen_x[None, :])
    shift = own_rho * eigen_y
    own_shift = lax.dynamic_slice_in_dim(shift, start, ROWS, 0)
    ends = jnp.stack([basis_z[0], basis_z[N - 1]])
    products = jnp.stack([ends[1] * ends[1], ends[1] * ends[0], ends[0] * ends[0]])
    products = jnp.pad(products, ((0, 13), (0, 0)))
    gram_x, gram_y = grams(basis_x, basis_y)

    part0 = forward(source, coarse, 0, basis_y, basis_z)
    pieces = faces(base_zx, shift, own_x, ends, products, part0, part1)
    following = from_behind(pieces[:, 2:4], "sub", -1)
    pieces, following, lines, gram_x, gram_y = lax.optimization_barrier(
        (pieces, following, lines, gram_x, gram_y)
    )
    spread = middle(base_xz, own_shift, basis_x, lines)
    shares = exchange(pieces[:, 0:2] - following)
    shares, spread = lax.optimization_barrier((shares, spread))
    own_jumps = jnp.sum(shares, axis=0)
    jumps = exchange(jnp.broadcast_to(own_jumps[None], (SLABS,) + own_jumps.shape))

    spread, jumps = lax.optimization_barrier((spread, jumps))
    spread = exchange(spread)

    first, image0, sums0 = chain0(
        weight.reshape(1), jumps, gram_x, gram_y, face_stiff, own_x, basis_y
    )
    before = from_behind(image0, "sub", 1)
    after = from_behind(image0, "sub", -1)

    terms = functools.partial(extra, base=base_xz, shift=shift, own_x=own_x, ends=ends)
    sums0 = over_pair(sums0)
    before, sums0 = lax.optimization_barrier((before, sums0))
    more = terms(0, own=image0, before=before)
    sums0, more = lax.optimization_barrier((over_pairs(sums0), more))
    alpha0 = step_length(sums0)

    scale = jnp.stack([alpha0, own_rho / next_rho, weight])
    sums1, jump, change = chain1(
        scale, jumps, image0, before, after, pieces, gram_x, gram_y, face_stiff, own_x, basis_y
    )
    sums1, more = lax.optimization_barrier((sums1, more))
    more = terms(1, own=image0, before=before, filled=(more,))
    sums1, more = lax.optimization_barrier((over_pair(sums1), more))
    more = terms(2, own=image0, before=before, filled=(more,))
    sums1, more = lax.optimization_barrier((over_pairs(sums1), more))
    alpha1 = step_length(sums1)
    multipliers = alpha0 * first + alpha1 * change
    solution = backward(scale, spread, more, basis_y, basis_z)
    return (solution[None], multipliers[None], jump[None])


def solution(mesh):
    in_specs = (
        P("sub", "slab", None, None),
        P(None, "sub", "slab", None, None),
        P(),
        P(),
        P(),
        P(),
        P(),
        P(),
        P(),
        P(),
    )
    out_specs = (P("sub", "slab", None, None), P("sub", "slab", None), P("sub", "slab", None))
    return jax.shard_map(
        on_device, mesh=mesh, in_specs=in_specs, out_specs=out_specs, check_vma=False
    )
```

```python
import functools

import jax
import jax.numpy as jnp
from jax import lax
from jax.experimental import pallas as pl
from jax.experimental.pallas import tpu as pltpu
from jax.sharding import PartitionSpec as P

HI = lax.Precision.HIGHEST
F32 = jnp.float32
BF16 = jnp.bfloat16
VMEM_LIMIT = 60 * 1024 * 1024
N = 256
ROWS = 16
SLABS = 16
LANES = 128
GROUP = 8
PARTS = ((0, 6), (6, 11), (11, 16))
BLOCK_COST = 15 * 10**8
FIELD = (SLABS, 2, N // SLABS, ROWS, LANES)


def params():
    return pltpu.CompilerParams(vmem_limit_bytes=VMEM_LIMIT)


def split(a):
    high = a.astype(BF16)
    low = (a - high.astype(F32)).astype(BF16)
    return high, low


def dot(a, b):
    return jnp.dot(a, b, preferred_element_type=F32)


def dot3(a, b):
    return dot(a[0], b[0]) + (dot(a[0], b[1]) + dot(a[1], b[0]))


def put_split(scratch, a):
    scratch[0], scratch[1] = split(a)


def whole(shape):
    return pl.BlockSpec(shape, lambda *_: (0,) * len(shape))


def smem():
    return pl.BlockSpec(memory_space=pltpu.SMEM)


def forward_kernel(source, coarse, basis_y, basis_z, out, left, right):
    step = pl.program_id(0)

    @pl.when(step == 0)
    def _():
        put_split(left, basis_y[...].T)
        put_split(right, basis_z[...])

    load = (source[...] + coarse[0, 0]).reshape(GROUP * N, N)
    first = dot3(split(load), right)
    for x in range(GROUP):
        part = dot3(left, split(first[x * N : x * N + N]))
        at = pl.ds((step * GROUP + x) % 8, ROWS, stride=8)
        for slab in range(SLABS):
            for half in range(2):
                rows = out.at[slab, half].reshape(ROWS * 8, LANES)
                piece = part[slab * ROWS : slab * ROWS + ROWS, LANES * half : LANES * half + LANES]
                rows[at, :] = piece


def forward(source, coarse, step, basis_y, basis_z):
    return pl.pallas_call(
        forward_kernel,
        grid=(ROWS // GROUP,),
        in_specs=[
            pl.BlockSpec((GROUP, N, N), lambda x: (x, 0, 0)),
            pl.BlockSpec((1, 1, GROUP, N, N), lambda x: (step, 0, x, 0, 0)),
            whole((N, N)),
            whole((N, N)),
        ],
        out_specs=pl.BlockSpec(
            (SLABS, 2, ROWS, 8, LANES), lambda x: (0, 0, 0, x * GROUP // 8, 0)
        ),
        out_shape=jax.ShapeDtypeStruct(FIELD, F32),
        scratch_shapes=[pltpu.VMEM((2, N, N), BF16), pltpu.VMEM((2, N, N), BF16)],
        compiler_params=params(),
        cost_estimate=pl.CostEstimate(
            flops=12 * ROWS * N**3, bytes_accessed=12 * ROWS * N * N, transcendentals=0
        ),
        name="forward",
    )(source, coarse, basis_y, basis_z)


def middle_kernel(base, shift, basis_x, lines, out, left, right):
    step = pl.program_id(0)

    @pl.when(step == 0)
    def _():
        put_split(left, basis_x[...].T)
        put_split(right, basis_x[...])

    for j in range(GROUP):
        halves = [lines[:, half, j].reshape(N, LANES) for half in range(2)]
        field = jnp.concatenate(halves, axis=1)
        modes = dot3(left, split(field)) / (base[...] + shift[step * GROUP + j])
        spread = dot3(right, split(modes))
        for half in range(2):
            piece = spread[:, LANES * half : LANES * half + LANES]
            out[:, half, j] = piece.reshape(SLABS, ROWS, LANES)


def middle(base, shift, basis_x, lines):
    block = pl.BlockSpec((SLABS, 2, GROUP, ROWS, LANES), lambda j: (0, 0, j, 0, 0))
    return pl.pallas_call(
        middle_kernel,
        grid=(N // SLABS // GROUP,),
        in_specs=[whole((N, N)), smem(), whole((N, N)), block],
        out_specs=block,
        out_shape=jax.ShapeDtypeStruct(FIELD, F32),
        scratch_shapes=[pltpu.VMEM((2, N, N), BF16), pltpu.VMEM((2, N, N), BF16)],
        compiler_params=params(),
        cost_estimate=pl.CostEstimate(
            flops=12 * ROWS * N**3, bytes_accessed=8 * ROWS * N * N, transcendentals=0
        ),
        name="middle",
    )(base, shift, basis_x, lines)


def backward_kernel(
    sums0, sums1, first, change, field, extra, basis_y, basis_z, out, multipliers, left, right
):
    step = pl.program_id(0)
    alpha = step_length(sums0[...])

    @pl.when(step == 0)
    def _():
        multipliers[...] = alpha * first[...] + step_length(sums1[...]) * change[...]
        put_split(left, basis_y[...])
        put_split(right, basis_z[...].T)

    def total(x, slab, half):
        at = pl.ds((step * GROUP + x) % 8, ROWS, stride=8)
        terms = [ref.at[slab, half].reshape(ROWS * 8, LANES)[at, :] for ref in (field, extra)]
        return terms[0] + alpha * terms[1]

    parts = []
    for x in range(GROUP):
        halves = [
            jnp.concatenate([total(x, slab, half) for slab in range(SLABS)], axis=0)
            for half in range(2)
        ]
        parts.append(dot3(left, split(jnp.concatenate(halves, axis=1))))
    part = jnp.concatenate(parts, axis=0)
    out[...] = dot3(split(part), right).reshape(GROUP, N, N)


def backward(sums0, sums1, first, change, field, extra, basis_y, basis_z):
    block = pl.BlockSpec((SLABS, 2, ROWS, 8, LANES), lambda x: (0, 0, 0, x * GROUP // 8, 0))
    return pl.pallas_call(
        backward_kernel,
        grid=(ROWS // GROUP,),
        in_specs=[
            whole((8, 128)),
            whole((8, 128)),
            whole((ROWS, N)),
            whole((ROWS, N)),
            block,
            block,
            whole((N, N)),
            whole((N, N)),
        ],
        out_specs=[pl.BlockSpec((GROUP, N, N), lambda x: (x, 0, 0)), whole((ROWS, N))],
        out_shape=[
            jax.ShapeDtypeStruct((ROWS, N, N), F32),
            jax.ShapeDtypeStruct((ROWS, N), F32),
        ],
        scratch_shapes=[pltpu.VMEM((2, N, N), BF16), pltpu.VMEM((2, N, N), BF16)],
        compiler_params=params(),
        cost_estimate=pl.CostEstimate(
            flops=12 * ROWS * N**3, bytes_accessed=12 * ROWS * N * N, transcendentals=0
        ),
        name="backward",
    )(sums0, sums1, first, change, field, extra, basis_y, basis_z)


def inverse_parts(denom):
    high = pl.reciprocal(denom, approx=True).astype(BF16)
    wide = high.astype(F32)
    low = (wide * (1.0 - denom * wide)).astype(BF16)
    return high, low


def times_inverse(rows, denom):
    high, low = split(rows)
    count = rows.shape[0]
    w_high, w_low = inverse_parts(denom)
    both = dot(jnp.concatenate([high, low], axis=0), w_high)
    return both[:count] + (both[count:] + dot(high, w_low))


def faces_kernel(
    own_rho, shift, eigen_x, eigen_z, own_x, basis_z, part0, part1, out, near, base, products
):
    block = pl.program_id(0)
    first, last = basis_z[0:1], basis_z[N - 1 : N]

    @pl.when(block == 0)
    def _():
        rows = jnp.broadcast_to(eigen_z[...], (N, N)).T
        base[...] = own_rho[0] * (rows + eigen_x[...])
        at = lax.broadcasted_iota(jnp.int32, (16, N), 0)
        products[...] = jnp.where(
            at == 0,
            last * last,
            jnp.where(at == 1, last * first, jnp.where(at == 2, first * first, 0.0)),
        )

    for jj in range(ROWS):
        a = jnp.concatenate([part0[0, 0, jj], part0[0, 1, jj]], axis=1)
        b = jnp.concatenate([part1[0, 0, jj], part1[0, 1, jj]], axis=1)
        rows = jnp.concatenate([a * last, b * last, a * first, b * first, products[...]], axis=0)
        result = dot3(split(rows), inverse_parts(base[...] + shift[block * ROWS + jj]))
        sums = [
            jnp.sum(result[16 * face : 16 * face + 16] * own_x[...], axis=0, keepdims=True)
            for face in range(4)
        ]
        for load in range(2):
            out[0, load, jj : jj + 1] = sums[load]
            near[0, load, jj : jj + 1] = sums[2 + load]
        for pair in range(3):
            out[0, 2 + pair, jj : jj + 1] = result[64 + pair : 65 + pair]


def faces(own_rho, shift, eigen_x, eigen_z, own_x, basis_z, part0, part1):
    block = pl.BlockSpec((1, 2, ROWS, ROWS, LANES), lambda j: (j, 0, 0, 0, 0))
    return pl.pallas_call(
        faces_kernel,
        grid=(SLABS,),
        in_specs=[
            smem(),
            smem(),
            whole((1, N)),
            whole((1, N)),
            whole((ROWS, N)),
            whole((N, N)),
            block,
            block,
        ],
        out_specs=[
            pl.BlockSpec((1, 5, ROWS, N), lambda j: (j, 0, 0, 0)),
            pl.BlockSpec((1, 2, ROWS, N), lambda j: (j, 0, 0, 0)),
        ],
        out_shape=[
            jax.ShapeDtypeStruct((SLABS, 5, ROWS, N), F32),
            jax.ShapeDtypeStruct((SLABS, 2, ROWS, N), F32),
        ],
        scratch_shapes=[pltpu.VMEM((N, N), F32), pltpu.VMEM((16, N), F32)],
        compiler_params=params(),
        cost_estimate=pl.CostEstimate(flops=N**3, bytes_accessed=N * N, transcendentals=0),
        name="faces",
    )(own_rho, shift, eigen_x, eigen_z, own_x, basis_z, part0, part1)


def extra_kernel(part, base, shift, own_x, ends, own, before, *refs):
    out = refs[-1]
    block = PARTS[part][0] + pl.program_id(0)
    first, last = ends[0:1], ends[1:2]
    for jj in range(ROWS):
        upper = own_x[...] * own[jj : jj + 1]
        lower = own_x[...] * before[jj : jj + 1]
        rows = jnp.concatenate([upper, lower], axis=0)
        result = times_inverse(rows, base[...] + shift[block * ROWS + jj])
        result = first * result[16:] - last * result[:16]
        for half in range(2):
            out[0, half, jj] = result[:, LANES * half : LANES * half + LANES]


def extra(part, base, shift, own_x, ends, own, before, filled=()):
    skip, stop = PARTS[part]
    return pl.pallas_call(
        functools.partial(extra_kernel, part),
        grid=(stop - skip,),
        in_specs=[
            whole((N, N)),
            smem(),
            whole((ROWS, N)),
            whole((2, N)),
            pl.BlockSpec((ROWS, N), lambda j: (skip + j, 0)),
            pl.BlockSpec((ROWS, N), lambda j: (skip + j, 0)),
        ]
        + [pl.BlockSpec(memory_space=pl.ANY)] * len(filled),
        out_specs=pl.BlockSpec((1, 2, ROWS, ROWS, LANES), lambda j: (skip + j, 0, 0, 0, 0)),
        out_shape=jax.ShapeDtypeStruct(FIELD, F32),
        input_output_aliases={6: 0} if filled else {},
        compiler_params=params(),
        cost_estimate=pl.CostEstimate(
            flops=BLOCK_COST * (stop - skip), bytes_accessed=N * N, transcendentals=0
        ),
        name=f"extra{part}",
    )(base, shift, own_x, ends, own, before, *filled)


def exact(a, b):
    return jnp.dot(a, b, precision=HI, preferred_element_type=F32)


def exact_t(a, b):
    dims = (((1,), (1,)), ((), ()))
    return lax.dot_general(a, b, dims, precision=HI, preferred_element_type=F32)


def precondition(jump, gram_x, gram_y, stiff):
    seen = exact(exact(gram_y, jump), gram_x)
    search = stiff * seen
    image = exact(exact(gram_y, search), gram_x)
    return search, image, jnp.sum(seen * search), jnp.sum(image * search)


def step_length(sums):
    return sums[0:1, 0:1] / (sums[1:2, 0:1] + 1e-06)


def scalars_block(upper, lower):
    at = lax.broadcasted_iota(jnp.int32, (8, 128), 0)
    return jnp.where(at == 0, upper, jnp.where(at == 1, lower, 0.0))


def chain0_kernel(scale, jumps, gram_x, gram_y, stiff, own_x, basis_y, rows, image, sums):
    search, image[...], upper, lower = precondition(
        jumps[:, 0].reshape(N, N), gram_x[...], gram_y[...], scale[0] * stiff[...].T
    )
    sums[...] = scalars_block(upper, lower)
    rows[...] = exact_t(exact_t(own_x[...], search), basis_y[...])


def chain0(*args):
    face = jax.ShapeDtypeStruct((N, N), F32)
    return pl.pallas_call(
        chain0_kernel,
        in_specs=[smem()] + [pl.BlockSpec(memory_space=pltpu.VMEM)] * 6,
        out_shape=(jax.ShapeDtypeStruct((ROWS, N), F32), face, jax.ShapeDtypeStruct((8, 128), F32)),
        compiler_params=params(),
        cost_estimate=pl.CostEstimate(
            flops=N**3, bytes_accessed=N * N, transcendentals=0
        ),
        name="chain0",
    )(*args)


def chain1_kernel(
    scale, sums_in, jumps, image, before, after, pieces, gram_x, gram_y, stiff, own_x, basis_y, sums, out, rows
):
    alpha, ratio, weight = step_length(sums_in[...]), scale[0], scale[1]
    t = image[...]
    table = [pieces[:, 2 + pair].reshape(N, N) for pair in range(3)]
    own = table[1] * before[...] - table[0] * t
    other = table[2] * t - table[1] * after[...]
    q = jumps[:, 1].reshape(N, N) + alpha * (own - ratio * other)
    search, _, upper, lower = precondition(
        q, gram_x[...], gram_y[...], weight * stiff[...].T
    )
    sums[...] = scalars_block(upper, lower)
    out[...] = exact_t(exact_t(own_x[...], q), basis_y[...])
    rows[...] = exact_t(exact_t(own_x[...], search), basis_y[...])


def chain1(*args):
    return pl.pallas_call(
        chain1_kernel,
        in_specs=[smem()] + [pl.BlockSpec(memory_space=pltpu.VMEM)] * 11,
        out_shape=(
            jax.ShapeDtypeStruct((8, 128), F32),
            jax.ShapeDtypeStruct((ROWS, N), F32),
            jax.ShapeDtypeStruct((ROWS, N), F32),
        ),
        compiler_params=params(),
        cost_estimate=pl.CostEstimate(
            flops=N**3, bytes_accessed=N * N, transcendentals=0
        ),
        name="chain1",
    )(*args)


def gram_kernel(basis_x, basis_y, gram_x, gram_y):
    gram_x[...] = exact(basis_x[...].T, basis_x[...])
    gram_y[...] = exact(basis_y[...].T, basis_y[...])


def grams(basis_x, basis_y):
    face = jax.ShapeDtypeStruct((N, N), F32)
    return pl.pallas_call(
        gram_kernel, out_shape=(face, face), compiler_params=params(), name="grams"
    )(basis_x, basis_y)


def from_behind(block, axis, distance):
    count = lax.axis_size(axis)
    route = [((i - distance) % count, i) for i in range(count)]
    return lax.ppermute(block, axis, route)


def from_partner(sums, bits):
    return lax.ppermute(sums, "sub", [(i, i ^ bits) for i in range(8)])


def over_pair(sums):
    return sums + from_partner(sums, 1)


def over_pairs(sums):
    return (sums + from_partner(sums, 2)) + (from_partner(sums, 4) + from_partner(sums, 6))


def exchange(block):
    return lax.all_to_all(block, "slab", split_axis=0, concat_axis=0, tiled=True)


def on_device(
    source, coarse, rho, basis_x, basis_y, basis_z, eigen_x, eigen_y, eigen_z, face_stiff
):
    source = source[0]
    sub_index = lax.axis_index("sub")
    slab_index = lax.axis_index("slab")
    subs = lax.axis_size("sub")
    own_rho = lax.dynamic_slice_in_dim(rho, sub_index, 1, 0)[0]
    next_rho = lax.dynamic_slice_in_dim(rho, (sub_index + 1) % subs, 1, 0)[0]
    weight = 0.5 * (own_rho + next_rho)
    start = slab_index * ROWS
    own_x = lax.dynamic_slice_in_dim(basis_x, start, ROWS, 0)

    own_shift = own_rho * lax.dynamic_slice_in_dim(eigen_y, start, ROWS, 0)
    shift = exchange(jnp.broadcast_to(own_shift, (SLABS, ROWS))).reshape(N)

    part1 = forward(source, coarse, 1, basis_y, basis_z)
    part1, shift = lax.optimization_barrier((part1, shift))
    lines = exchange(part1)

    base_xz = own_rho * (eigen_x[:, None] + eigen_z[None, :])
    ends = jnp.stack([basis_z[0], basis_z[N - 1]])
    gram_x, gram_y = grams(basis_x, basis_y)

    part0 = forward(source, coarse, 0, basis_y, basis_z)
    pieces, near = faces(
        own_rho.reshape(1), shift, eigen_x[None], eigen_z[None], own_x, basis_z, part0, part1
    )
    shares = pieces[:, 0:2] - from_behind(near, "sub", -1)
    shares, lines, gram_x, gram_y, base_xz, ends = lax.optimization_barrier(
        (shares, lines, gram_x, gram_y, base_xz, ends)
    )
    spread = middle(base_xz, own_shift, basis_x, lines)
    shares = exchange(shares)
    shares, spread = lax.optimization_barrier((shares, spread))
    own_jumps = jnp.sum(shares, axis=0)
    jumps = exchange(jnp.broadcast_to(own_jumps[None], (SLABS,) + own_jumps.shape))
    spread, jumps = lax.optimization_barrier((spread, jumps))
    spread = exchange(spread)

    first, image0, sums0 = chain0(
        weight.reshape(1), jumps, gram_x, gram_y, face_stiff, own_x, basis_y
    )
    before = from_behind(image0, "sub", 1)
    after = from_behind(image0, "sub", -1)

    terms = functools.partial(extra, base=base_xz, shift=shift, own_x=own_x, ends=ends)
    sums0 = over_pair(sums0)
    before, sums0 = lax.optimization_barrier((before, sums0))
    more = terms(0, own=image0, before=before)
    sums0, more = lax.optimization_barrier((over_pairs(sums0), more))

    scale = jnp.stack([own_rho / next_rho, weight])
    sums1, jump, change = chain1(
        scale,
        sums0,
        jumps,
        image0,
        before,
        after,
        pieces,
        gram_x,
        gram_y,
        face_stiff,
        own_x,
        basis_y,
    )
    sums1, more = lax.optimization_barrier((sums1, more))
    more = terms(1, own=image0, before=before, filled=(more,))
    sums1, more = lax.optimization_barrier((over_pair(sums1), more))
    more = terms(2, own=image0, before=before, filled=(more,))
    sums1, more = lax.optimization_barrier((over_pairs(sums1), more))
    solution, multipliers = backward(
        sums0, sums1, first, change, spread, more, basis_y, basis_z
    )
    return (solution[None], multipliers[None], jump[None])


def solution(mesh):
    in_specs = (
        P("sub", "slab", None, None),
        P(None, "sub", "slab", None, None),
        P(),
        P(),
        P(),
        P(),
        P(),
        P(),
        P(),
        P(),
    )
    out_specs = (P("sub", "slab", None, None), P("sub", "slab", None), P("sub", "slab", None))
    return jax.shard_map(
        on_device, mesh=mesh, in_specs=in_specs, out_specs=out_specs, check_vma=False
    )
```

```python
import functools

import jax
import jax.numpy as jnp
from jax import lax
from jax.experimental import pallas as pl
from jax.experimental.pallas import tpu as pltpu
from jax.sharding import PartitionSpec as P

HI = lax.Precision.HIGHEST
F32 = jnp.float32
BF16 = jnp.bfloat16
VMEM_LIMIT = 60 * 1024 * 1024
N = 256
ROWS = 16
SLABS = 16
LANES = 128
GROUP = 8
PARTS = ((0, 6), (6, 11), (11, 16))
BLOCK_COST = 15 * 10**8
FIELD = (SLABS, 2, N // SLABS, ROWS, LANES)


def params():
    return pltpu.CompilerParams(vmem_limit_bytes=VMEM_LIMIT)


def split(a):
    high = a.astype(BF16)
    low = (a - high.astype(F32)).astype(BF16)
    return high, low


def dot(a, b):
    return jnp.dot(a, b, preferred_element_type=F32)


def dot3(a, b):
    return dot(a[0], b[0]) + (dot(a[0], b[1]) + dot(a[1], b[0]))


def put_split(scratch, a):
    scratch[0], scratch[1] = split(a)


def whole(shape):
    return pl.BlockSpec(shape, lambda *_: (0,) * len(shape))


def smem():
    return pl.BlockSpec(memory_space=pltpu.SMEM)


def forward_kernel(source, coarse, basis_y, basis_z, out, left, right):
    step = pl.program_id(0)

    @pl.when(step == 0)
    def _():
        put_split(left, basis_y[...].T)
        put_split(right, basis_z[...])

    load = (source[...] + coarse[0, 0]).reshape(GROUP * N, N)
    first = dot3(split(load), right)
    for x in range(GROUP):
        part = dot3(left, split(first[x * N : x * N + N]))
        at = pl.ds((step * GROUP + x) % 8, ROWS, stride=8)
        for slab in range(SLABS):
            for half in range(2):
                rows = out.at[slab, half].reshape(ROWS * 8, LANES)
                piece = part[slab * ROWS : slab * ROWS + ROWS, LANES * half : LANES * half + LANES]
                rows[at, :] = piece


def forward(source, coarse, step, basis_y, basis_z):
    return pl.pallas_call(
        forward_kernel,
        grid=(ROWS // GROUP,),
        in_specs=[
            pl.BlockSpec((GROUP, N, N), lambda x: (x, 0, 0)),
            pl.BlockSpec((1, 1, GROUP, N, N), lambda x: (step, 0, x, 0, 0)),
            whole((N, N)),
            whole((N, N)),
        ],
        out_specs=pl.BlockSpec(
            (SLABS, 2, ROWS, 8, LANES), lambda x: (0, 0, 0, x * GROUP // 8, 0)
        ),
        out_shape=jax.ShapeDtypeStruct(FIELD, F32),
        scratch_shapes=[pltpu.VMEM((2, N, N), BF16), pltpu.VMEM((2, N, N), BF16)],
        compiler_params=params(),
        cost_estimate=pl.CostEstimate(
            flops=12 * ROWS * N**3, bytes_accessed=12 * ROWS * N * N, transcendentals=0
        ),
        name="forward",
    )(source, coarse, basis_y, basis_z)


def middle_kernel(base, shift, basis_x, lines, out, left, right):
    step = pl.program_id(0)

    @pl.when(step == 0)
    def _():
        put_split(left, basis_x[...].T)
        put_split(right, basis_x[...])

    for j in range(GROUP):
        halves = [lines[:, half, j].reshape(N, LANES) for half in range(2)]
        field = jnp.concatenate(halves, axis=1)
        modes = dot3(left, split(field)) / (base[...] + shift[step * GROUP + j])
        spread = dot3(right, split(modes))
        for half in range(2):
            piece = spread[:, LANES * half : LANES * half + LANES]
            out[:, half, j] = piece.reshape(SLABS, ROWS, LANES)


def middle(base, shift, basis_x, lines):
    block = pl.BlockSpec((SLABS, 2, GROUP, ROWS, LANES), lambda j: (0, 0, j, 0, 0))
    return pl.pallas_call(
        middle_kernel,
        grid=(N // SLABS // GROUP,),
        in_specs=[whole((N, N)), smem(), whole((N, N)), block],
        out_specs=block,
        out_shape=jax.ShapeDtypeStruct(FIELD, F32),
        scratch_shapes=[pltpu.VMEM((2, N, N), BF16), pltpu.VMEM((2, N, N), BF16)],
        compiler_params=params(),
        cost_estimate=pl.CostEstimate(
            flops=12 * ROWS * N**3, bytes_accessed=8 * ROWS * N * N, transcendentals=0
        ),
        name="middle",
    )(base, shift, basis_x, lines)


def backward_kernel(
    sums0, sums1, first, change, field, extra, basis_y, basis_z, out, multipliers, left, right
):
    step = pl.program_id(0)
    alpha = step_length(sums0[...])

    @pl.when(step == 0)
    def _():
        multipliers[...] = alpha * first[...] + step_length(sums1[...]) * change[...]
        put_split(left, basis_y[...])
        put_split(right, basis_z[...].T)

    def total(x, slab, half):
        at = pl.ds((step * GROUP + x) % 8, ROWS, stride=8)
        terms = [ref.at[slab, half].reshape(ROWS * 8, LANES)[at, :] for ref in (field, extra)]
        return terms[0] + alpha * terms[1]

    parts = []
    for x in range(GROUP):
        halves = [
            jnp.concatenate([total(x, slab, half) for slab in range(SLABS)], axis=0)
            for half in range(2)
        ]
        parts.append(dot3(left, split(jnp.concatenate(halves, axis=1))))
    part = jnp.concatenate(parts, axis=0)
    out[...] = dot3(split(part), right).reshape(GROUP, N, N)


def backward(sums0, sums1, first, change, field, extra, basis_y, basis_z):
    block = pl.BlockSpec((SLABS, 2, ROWS, 8, LANES), lambda x: (0, 0, 0, x * GROUP // 8, 0))
    return pl.pallas_call(
        backward_kernel,
        grid=(ROWS // GROUP,),
        in_specs=[
            whole((8, 128)),
            whole((8, 128)),
            whole((ROWS, N)),
            whole((ROWS, N)),
            block,
            block,
            whole((N, N)),
            whole((N, N)),
        ],
        out_specs=[pl.BlockSpec((GROUP, N, N), lambda x: (x, 0, 0)), whole((ROWS, N))],
        out_shape=[
            jax.ShapeDtypeStruct((ROWS, N, N), F32),
            jax.ShapeDtypeStruct((ROWS, N), F32),
        ],
        scratch_shapes=[pltpu.VMEM((2, N, N), BF16), pltpu.VMEM((2, N, N), BF16)],
        compiler_params=params(),
        cost_estimate=pl.CostEstimate(
            flops=12 * ROWS * N**3, bytes_accessed=12 * ROWS * N * N, transcendentals=0
        ),
        name="backward",
    )(sums0, sums1, first, change, field, extra, basis_y, basis_z)


def inverse_parts(denom):
    high = pl.reciprocal(denom, approx=True).astype(BF16)
    wide = high.astype(F32)
    low = (wide * (1.0 - denom * wide)).astype(BF16)
    return high, low


def times_inverse(rows, denom):
    high, low = split(rows)
    count = rows.shape[0]
    w_high, w_low = inverse_parts(denom)
    both = dot(jnp.concatenate([high, low], axis=0), w_high)
    return both[:count] + (both[count:] + dot(high, w_low))


def faces_kernel(
    own_rho, shift, eigen_x, eigen_z, own_x, basis_z, part0, part1, out, near, base, products
):
    block = pl.program_id(0)
    first, last = basis_z[0:1], basis_z[N - 1 : N]

    @pl.when(block == 0)
    def _():
        rows = jnp.broadcast_to(eigen_z[...], (N, N)).T
        base[...] = own_rho[0] * (rows + eigen_x[...])
        at = lax.broadcasted_iota(jnp.int32, (16, N), 0)
        products[...] = jnp.where(
            at == 0,
            last * last,
            jnp.where(at == 1, last * first, jnp.where(at == 2, first * first, 0.0)),
        )

    for jj in range(ROWS):
        a = jnp.concatenate([part0[0, 0, jj], part0[0, 1, jj]], axis=1)
        b = jnp.concatenate([part1[0, 0, jj], part1[0, 1, jj]], axis=1)
        rows = jnp.concatenate([a * last, b * last, a * first, b * first, products[...]], axis=0)
        result = dot3(split(rows), inverse_parts(base[...] + shift[block * ROWS + jj]))
        sums = [
            jnp.sum(result[16 * face : 16 * face + 16] * own_x[...], axis=0, keepdims=True)
            for face in range(4)
        ]
        for load in range(2):
            out[0, load, jj : jj + 1] = sums[load]
            near[0, load, jj : jj + 1] = sums[2 + load]
        for pair in range(3):
            out[0, 2 + pair, jj : jj + 1] = result[64 + pair : 65 + pair]


def faces(own_rho, shift, eigen_x, eigen_z, own_x, basis_z, part0, part1):
    block = pl.BlockSpec((1, 2, ROWS, ROWS, LANES), lambda j: (j, 0, 0, 0, 0))
    return pl.pallas_call(
        faces_kernel,
        grid=(SLABS,),
        in_specs=[
            smem(),
            smem(),
            whole((1, N)),
            whole((1, N)),
            whole((ROWS, N)),
            whole((N, N)),
            block,
            block,
        ],
        out_specs=[
            pl.BlockSpec((1, 5, ROWS, N), lambda j: (j, 0, 0, 0)),
            pl.BlockSpec((1, 2, ROWS, N), lambda j: (j, 0, 0, 0)),
        ],
        out_shape=[
            jax.ShapeDtypeStruct((SLABS, 5, ROWS, N), F32),
            jax.ShapeDtypeStruct((SLABS, 2, ROWS, N), F32),
        ],
        scratch_shapes=[pltpu.VMEM((N, N), F32), pltpu.VMEM((16, N), F32)],
        compiler_params=params(),
        cost_estimate=pl.CostEstimate(flops=N**3, bytes_accessed=N * N, transcendentals=0),
        name="faces",
    )(own_rho, shift, eigen_x, eigen_z, own_x, basis_z, part0, part1)


def extra_kernel(part, base, shift, own_x, ends, own, before, *refs):
    out = refs[-1]
    block = PARTS[part][0] + pl.program_id(0)
    first, last = ends[0:1], ends[1:2]
    for jj in range(ROWS):
        upper = own_x[...] * own[jj : jj + 1]
        lower = own_x[...] * before[jj : jj + 1]
        rows = jnp.concatenate([upper, lower], axis=0)
        result = times_inverse(rows, base[...] + shift[block * ROWS + jj])
        result = first * result[16:] - last * result[:16]
        for half in range(2):
            out[0, half, jj] = result[:, LANES * half : LANES * half + LANES]


def extra(part, base, shift, own_x, ends, own, before, filled=()):
    skip, stop = PARTS[part]
    return pl.pallas_call(
        functools.partial(extra_kernel, part),
        grid=(stop - skip,),
        in_specs=[
            whole((N, N)),
            smem(),
            whole((ROWS, N)),
            whole((2, N)),
            pl.BlockSpec((ROWS, N), lambda j: (skip + j, 0)),
            pl.BlockSpec((ROWS, N), lambda j: (skip + j, 0)),
        ]
        + [pl.BlockSpec(memory_space=pl.ANY)] * len(filled),
        out_specs=pl.BlockSpec((1, 2, ROWS, ROWS, LANES), lambda j: (skip + j, 0, 0, 0, 0)),
        out_shape=jax.ShapeDtypeStruct(FIELD, F32),
        input_output_aliases={6: 0} if filled else {},
        compiler_params=params(),
        cost_estimate=pl.CostEstimate(
            flops=BLOCK_COST * (stop - skip), bytes_accessed=N * N, transcendentals=0
        ),
        name=f"extra{part}",
    )(base, shift, own_x, ends, own, before, *filled)


def exact(a, b):
    return jnp.dot(a, b, precision=HI, preferred_element_type=F32)


def exact_t(a, b):
    dims = (((1,), (1,)), ((), ()))
    return lax.dot_general(a, b, dims, precision=HI, preferred_element_type=F32)


def precondition(jump, gram_x, gram_y, stiff):
    seen = exact(exact(gram_y, jump), gram_x)
    search = stiff * seen
    image = exact(exact(gram_y, search), gram_x)
    return search, image, jnp.sum(seen * search), jnp.sum(image * search)


def step_length(sums):
    return sums[0:1, 0:1] / (sums[1:2, 0:1] + 1e-06)


def scalars_block(upper, lower):
    at = lax.broadcasted_iota(jnp.int32, (8, 128), 0)
    return jnp.where(at == 0, upper, jnp.where(at == 1, lower, 0.0))


def chain0_kernel(scale, jumps, gram_x, gram_y, stiff, own_x, basis_y, rows, image, sums):
    search, image[...], upper, lower = precondition(
        jumps[:, 0].reshape(N, N), gram_x[...], gram_y[...], scale[0] * stiff[...].T
    )
    sums[...] = scalars_block(upper, lower)
    rows[...] = exact_t(exact_t(own_x[...], search), basis_y[...])


def chain0(*args):
    face = jax.ShapeDtypeStruct((N, N), F32)
    return pl.pallas_call(
        chain0_kernel,
        in_specs=[smem()] + [pl.BlockSpec(memory_space=pltpu.VMEM)] * 6,
        out_shape=(jax.ShapeDtypeStruct((ROWS, N), F32), face, jax.ShapeDtypeStruct((8, 128), F32)),
        compiler_params=params(),
        cost_estimate=pl.CostEstimate(
            flops=N**3, bytes_accessed=N * N, transcendentals=0
        ),
        name="chain0",
    )(*args)


def chain1_kernel(
    scale, sums_in, jumps, image, before, after, pieces, gram_x, gram_y, stiff, own_x, basis_y, sums, out, rows
):
    alpha, ratio, weight = step_length(sums_in[...]), scale[0], scale[1]
    t = image[...]
    table = [pieces[:, 2 + pair].reshape(N, N) for pair in range(3)]
    own = table[1] * before[...] - table[0] * t
    other = table[2] * t - table[1] * after[...]
    q = jumps[:, 1].reshape(N, N) + alpha * (own - ratio * other)
    search, _, upper, lower = precondition(
        q, gram_x[...], gram_y[...], weight * stiff[...].T
    )
    sums[...] = scalars_block(upper, lower)
    out[...] = exact_t(exact_t(own_x[...], q), basis_y[...])
    rows[...] = exact_t(exact_t(own_x[...], search), basis_y[...])


def chain1(*args):
    return pl.pallas_call(
        chain1_kernel,
        in_specs=[smem()] + [pl.BlockSpec(memory_space=pltpu.VMEM)] * 11,
        out_shape=(
            jax.ShapeDtypeStruct((8, 128), F32),
            jax.ShapeDtypeStruct((ROWS, N), F32),
            jax.ShapeDtypeStruct((ROWS, N), F32),
        ),
        compiler_params=params(),
        cost_estimate=pl.CostEstimate(
            flops=N**3, bytes_accessed=N * N, transcendentals=0
        ),
        name="chain1",
    )(*args)


def gram_kernel(basis_x, basis_y, gram_x, gram_y):
    gram_x[...] = exact(basis_x[...].T, basis_x[...])
    gram_y[...] = exact(basis_y[...].T, basis_y[...])


def grams(basis_x, basis_y):
    face = jax.ShapeDtypeStruct((N, N), F32)
    return pl.pallas_call(
        gram_kernel, out_shape=(face, face), compiler_params=params(), name="grams"
    )(basis_x, basis_y)


def from_behind(block, axis, distance):
    count = lax.axis_size(axis)
    route = [((i - distance) % count, i) for i in range(count)]
    return lax.ppermute(block, axis, route)


def from_partner(sums, bits):
    return lax.ppermute(sums, "sub", [(i, i ^ bits) for i in range(8)])


def over_pair(sums):
    return sums + from_partner(sums, 1)


def over_pairs(sums):
    return (sums + from_partner(sums, 2)) + (from_partner(sums, 4) + from_partner(sums, 6))


def exchange(block):
    return lax.all_to_all(block, "slab", split_axis=0, concat_axis=0, tiled=True)


def on_device(
    source, coarse, rho, basis_x, basis_y, basis_z, eigen_x, eigen_y, eigen_z, face_stiff
):
    source = source[0]
    sub_index = lax.axis_index("sub")
    slab_index = lax.axis_index("slab")
    subs = lax.axis_size("sub")
    own_rho = lax.dynamic_slice_in_dim(rho, sub_index, 1, 0)[0]
    next_rho = lax.dynamic_slice_in_dim(rho, (sub_index + 1) % subs, 1, 0)[0]
    weight = 0.5 * (own_rho + next_rho)
    start = slab_index * ROWS
    own_x = lax.dynamic_slice_in_dim(basis_x, start, ROWS, 0)

    part1 = forward(source, coarse, 1, basis_y, basis_z)
    lines = exchange(part1)

    shift = own_rho * eigen_y
    own_shift = lax.dynamic_slice_in_dim(shift, start, ROWS, 0)
    base_xz = own_rho * (eigen_x[:, None] + eigen_z[None, :])
    ends = jnp.stack([basis_z[0], basis_z[N - 1]])
    gram_x, gram_y = grams(basis_x, basis_y)

    part0 = forward(source, coarse, 0, basis_y, basis_z)
    pieces, near = faces(
        own_rho.reshape(1), shift, eigen_x[None], eigen_z[None], own_x, basis_z, part0, part1
    )
    shares = pieces[:, 0:2] - from_behind(near, "sub", -1)
    shares, lines, gram_x, gram_y, base_xz, ends = lax.optimization_barrier(
        (shares, lines, gram_x, gram_y, base_xz, ends)
    )
    spread = middle(base_xz, own_shift, basis_x, lines)
    shares = exchange(shares)
    shares, spread = lax.optimization_barrier((shares, spread))
    own_jumps = jnp.sum(shares, axis=0)
    jumps = exchange(jnp.broadcast_to(own_jumps[None], (SLABS,) + own_jumps.shape))
    spread, jumps = lax.optimization_barrier((spread, jumps))
    spread = exchange(spread)

    first, image0, sums0 = chain0(
        weight.reshape(1), jumps, gram_x, gram_y, face_stiff, own_x, basis_y
    )
    before = from_behind(image0, "sub", 1)
    after = from_behind(image0, "sub", -1)

    terms = functools.partial(extra, base=base_xz, shift=shift, own_x=own_x, ends=ends)
    sums0 = over_pair(sums0)
    before, sums0 = lax.optimization_barrier((before, sums0))
    more = terms(0, own=image0, before=before)
    sums0, more = lax.optimization_barrier((over_pairs(sums0), more))

    scale = jnp.stack([own_rho / next_rho, weight])
    sums1, jump, change = chain1(
        scale,
        sums0,
        jumps,
        image0,
        before,
        after,
        pieces,
        gram_x,
        gram_y,
        face_stiff,
        own_x,
        basis_y,
    )
    sums1, more = lax.optimization_barrier((sums1, more))
    more = terms(1, own=image0, before=before, filled=(more,))
    sums1, more = lax.optimization_barrier((over_pair(sums1), more))
    more = terms(2, own=image0, before=before, filled=(more,))
    sums1, more = lax.optimization_barrier((over_pairs(sums1), more))
    solution, multipliers = backward(
        sums0, sums1, first, change, spread, more, basis_y, basis_z
    )
    return (solution[None], multipliers[None], jump[None])


def solution(mesh):
    in_specs = (
        P("sub", "slab", None, None),
        P(None, "sub", "slab", None, None),
        P(),
        P(),
        P(),
        P(),
        P(),
        P(),
        P(),
        P(),
    )
    out_specs = (P("sub", "slab", None, None), P("sub", "slab", None), P("sub", "slab", None))
    return jax.shard_map(
        on_device, mesh=mesh, in_specs=in_specs, out_specs=out_specs, check_vma=False
    )
```

```python
import functools

import jax
import jax.numpy as jnp
from jax import lax
from jax.experimental import pallas as pl
from jax.experimental.pallas import tpu as pltpu
from jax.sharding import PartitionSpec as P

HI = lax.Precision.HIGHEST
F32 = jnp.float32
BF16 = jnp.bfloat16
VMEM_LIMIT = 60 * 1024 * 1024
N = 256
ROWS = 16
SLABS = 16
LANES = 128
GROUP = 8
PARTS = ((0, 6), (6, 11), (11, 16))
BLOCK_COST = 15 * 10**8
FIELD = (SLABS, 2, N // SLABS, ROWS, LANES)


def params():
    return pltpu.CompilerParams(vmem_limit_bytes=VMEM_LIMIT)


def split(a):
    high = a.astype(BF16)
    low = (a - high.astype(F32)).astype(BF16)
    return high, low


def dot(a, b):
    return jnp.dot(a, b, preferred_element_type=F32)


def dot3(a, b):
    return dot(a[0], b[0]) + (dot(a[0], b[1]) + dot(a[1], b[0]))


def put_split(scratch, a):
    scratch[0], scratch[1] = split(a)


def whole(shape):
    return pl.BlockSpec(shape, lambda *_: (0,) * len(shape))


def smem():
    return pl.BlockSpec(memory_space=pltpu.SMEM)


def forward_kernel(source, coarse, basis_y, basis_z, out, left, right):
    step = pl.program_id(0)

    @pl.when(step == 0)
    def _():
        put_split(left, basis_y[...].T)
        put_split(right, basis_z[...])

    load = (source[...] + coarse[0, 0]).reshape(GROUP * N, N)
    first = dot3(split(load), right)
    for x in range(GROUP):
        part = dot3(left, split(first[x * N : x * N + N]))
        at = pl.ds((step * GROUP + x) % 8, ROWS, stride=8)
        for slab in range(SLABS):
            for half in range(2):
                rows = out.at[slab, half].reshape(ROWS * 8, LANES)
                piece = part[slab * ROWS : slab * ROWS + ROWS, LANES * half : LANES * half + LANES]
                rows[at, :] = piece


def forward(source, coarse, step, basis_y, basis_z):
    return pl.pallas_call(
        forward_kernel,
        grid=(ROWS // GROUP,),
        in_specs=[
            pl.BlockSpec((GROUP, N, N), lambda x: (x, 0, 0)),
            pl.BlockSpec((1, 1, GROUP, N, N), lambda x: (step, 0, x, 0, 0)),
            whole((N, N)),
            whole((N, N)),
        ],
        out_specs=pl.BlockSpec(
            (SLABS, 2, ROWS, 8, LANES), lambda x: (0, 0, 0, x * GROUP // 8, 0)
        ),
        out_shape=jax.ShapeDtypeStruct(FIELD, F32),
        scratch_shapes=[pltpu.VMEM((2, N, N), BF16), pltpu.VMEM((2, N, N), BF16)],
        compiler_params=params(),
        cost_estimate=pl.CostEstimate(
            flops=12 * ROWS * N**3, bytes_accessed=12 * ROWS * N * N, transcendentals=0
        ),
        name="forward",
    )(source, coarse, basis_y, basis_z)


def middle_kernel(base, shift, basis_x, lines, out, left, right):
    step = pl.program_id(0)

    @pl.when(step == 0)
    def _():
        put_split(left, basis_x[...].T)
        put_split(right, basis_x[...])

    for j in range(GROUP):
        halves = [lines[:, half, j].reshape(N, LANES) for half in range(2)]
        field = jnp.concatenate(halves, axis=1)
        modes = dot3(left, split(field)) / (base[...] + shift[step * GROUP + j])
        spread = dot3(right, split(modes))
        for half in range(2):
            piece = spread[:, LANES * half : LANES * half + LANES]
            out[:, half, j] = piece.reshape(SLABS, ROWS, LANES)


def middle(base, shift, basis_x, lines):
    block = pl.BlockSpec((SLABS, 2, GROUP, ROWS, LANES), lambda j: (0, 0, j, 0, 0))
    return pl.pallas_call(
        middle_kernel,
        grid=(N // SLABS // GROUP,),
        in_specs=[whole((N, N)), smem(), whole((N, N)), block],
        out_specs=block,
        out_shape=jax.ShapeDtypeStruct(FIELD, F32),
        scratch_shapes=[pltpu.VMEM((2, N, N), BF16), pltpu.VMEM((2, N, N), BF16)],
        compiler_params=params(),
        cost_estimate=pl.CostEstimate(
            flops=12 * ROWS * N**3, bytes_accessed=8 * ROWS * N * N, transcendentals=0
        ),
        name="middle",
    )(base, shift, basis_x, lines)


def backward_kernel(
    sums0, sums1, first, change, field, extra, basis_y, basis_z, out, multipliers, left, right
):
    step = pl.program_id(0)
    alpha = step_length(sums0[...])

    @pl.when(step == 0)
    def _():
        multipliers[...] = alpha * first[...] + step_length(sums1[...]) * change[...]
        put_split(left, basis_y[...])
        put_split(right, basis_z[...].T)

    def total(x, slab, half):
        at = pl.ds((step * GROUP + x) % 8, ROWS, stride=8)
        terms = [ref.at[slab, half].reshape(ROWS * 8, LANES)[at, :] for ref in (field, extra)]
        return terms[0] + alpha * terms[1]

    parts = []
    for x in range(GROUP):
        halves = [
            jnp.concatenate([total(x, slab, half) for slab in range(SLABS)], axis=0)
            for half in range(2)
        ]
        parts.append(dot3(left, split(jnp.concatenate(halves, axis=1))))
    part = jnp.concatenate(parts, axis=0)
    out[...] = dot3(split(part), right).reshape(GROUP, N, N)


def backward(sums0, sums1, first, change, field, extra, basis_y, basis_z):
    block = pl.BlockSpec((SLABS, 2, ROWS, 8, LANES), lambda x: (0, 0, 0, x * GROUP // 8, 0))
    return pl.pallas_call(
        backward_kernel,
        grid=(ROWS // GROUP,),
        in_specs=[
            whole((8, N)),
            whole((8, N)),
            whole((ROWS, N)),
            whole((ROWS, N)),
            block,
            block,
            whole((N, N)),
            whole((N, N)),
        ],
        out_specs=[pl.BlockSpec((GROUP, N, N), lambda x: (x, 0, 0)), whole((ROWS, N))],
        out_shape=[
            jax.ShapeDtypeStruct((ROWS, N, N), F32),
            jax.ShapeDtypeStruct((ROWS, N), F32),
        ],
        scratch_shapes=[pltpu.VMEM((2, N, N), BF16), pltpu.VMEM((2, N, N), BF16)],
        compiler_params=params(),
        cost_estimate=pl.CostEstimate(
            flops=12 * ROWS * N**3, bytes_accessed=12 * ROWS * N * N, transcendentals=0
        ),
        name="backward",
    )(sums0, sums1, first, change, field, extra, basis_y, basis_z)


def inverse_parts(denom):
    high = pl.reciprocal(denom, approx=True).astype(BF16)
    wide = high.astype(F32)
    low = (wide * (1.0 - denom * wide)).astype(BF16)
    return high, low


def times_inverse(rows, denom):
    high, low = split(rows)
    count = rows.shape[0]
    w_high, w_low = inverse_parts(denom)
    both = dot(jnp.concatenate([high, low], axis=0), w_high)
    return both[:count] + (both[count:] + dot(high, w_low))


def faces_kernel(
    own_rho, shift, eigen_x, eigen_z, own_x, basis_z, part0, part1, out, near, base, products
):
    block = pl.program_id(0)
    first, last = basis_z[0:1], basis_z[N - 1 : N]

    @pl.when(block == 0)
    def _():
        rows = jnp.broadcast_to(eigen_z[...], (N, N)).T
        base[...] = own_rho[0] * (rows + eigen_x[...])
        at = lax.broadcasted_iota(jnp.int32, (16, N), 0)
        products[...] = jnp.where(
            at == 0,
            last * last,
            jnp.where(at == 1, last * first, jnp.where(at == 2, first * first, 0.0)),
        )

    for jj in range(ROWS):
        a = jnp.concatenate([part0[0, 0, jj], part0[0, 1, jj]], axis=1)
        b = jnp.concatenate([part1[0, 0, jj], part1[0, 1, jj]], axis=1)
        rows = jnp.concatenate([a * last, b * last, a * first, b * first, products[...]], axis=0)
        result = dot3(split(rows), inverse_parts(base[...] + shift[block * ROWS + jj]))
        sums = [
            jnp.sum(result[16 * face : 16 * face + 16] * own_x[...], axis=0, keepdims=True)
            for face in range(4)
        ]
        for load in range(2):
            out[0, load, jj : jj + 1] = sums[load]
            near[0, load, jj : jj + 1] = sums[2 + load]
        for pair in range(3):
            out[0, 2 + pair, jj : jj + 1] = result[64 + pair : 65 + pair]


def faces(own_rho, shift, eigen_x, eigen_z, own_x, basis_z, part0, part1):
    block = pl.BlockSpec((1, 2, ROWS, ROWS, LANES), lambda j: (j, 0, 0, 0, 0))
    return pl.pallas_call(
        faces_kernel,
        grid=(SLABS,),
        in_specs=[
            smem(),
            smem(),
            whole((1, N)),
            whole((1, N)),
            whole((ROWS, N)),
            whole((N, N)),
            block,
            block,
        ],
        out_specs=[
            pl.BlockSpec((1, 5, ROWS, N), lambda j: (j, 0, 0, 0)),
            pl.BlockSpec((1, 2, ROWS, N), lambda j: (j, 0, 0, 0)),
        ],
        out_shape=[
            jax.ShapeDtypeStruct((SLABS, 5, ROWS, N), F32),
            jax.ShapeDtypeStruct((SLABS, 2, ROWS, N), F32),
        ],
        scratch_shapes=[pltpu.VMEM((N, N), F32), pltpu.VMEM((16, N), F32)],
        compiler_params=params(),
        cost_estimate=pl.CostEstimate(flops=N**3, bytes_accessed=N * N, transcendentals=0),
        name="faces",
    )(own_rho, shift, eigen_x, eigen_z, own_x, basis_z, part0, part1)


def extra_kernel(part, base, shift, own_x, ends, own, before, *refs):
    out = refs[-1]
    block = PARTS[part][0] + pl.program_id(0)
    first, last = ends[0:1], ends[1:2]
    for jj in range(ROWS):
        upper = own_x[...] * own[jj : jj + 1]
        lower = own_x[...] * before[jj : jj + 1]
        rows = jnp.concatenate([upper, lower], axis=0)
        result = times_inverse(rows, base[...] + shift[block * ROWS + jj])
        result = first * result[16:] - last * result[:16]
        for half in range(2):
            out[0, half, jj] = result[:, LANES * half : LANES * half + LANES]


def extra(part, base, shift, own_x, ends, own, before, filled=()):
    skip, stop = PARTS[part]
    return pl.pallas_call(
        functools.partial(extra_kernel, part),
        grid=(stop - skip,),
        in_specs=[
            whole((N, N)),
            smem(),
            whole((ROWS, N)),
            whole((2, N)),
            pl.BlockSpec((ROWS, N), lambda j: (skip + j, 0)),
            pl.BlockSpec((ROWS, N), lambda j: (skip + j, 0)),
        ]
        + [pl.BlockSpec(memory_space=pl.ANY)] * len(filled),
        out_specs=pl.BlockSpec((1, 2, ROWS, ROWS, LANES), lambda j: (skip + j, 0, 0, 0, 0)),
        out_shape=jax.ShapeDtypeStruct(FIELD, F32),
        input_output_aliases={6: 0} if filled else {},
        compiler_params=params(),
        cost_estimate=pl.CostEstimate(
            flops=BLOCK_COST * (stop - skip), bytes_accessed=N * N, transcendentals=0
        ),
        name=f"extra{part}",
    )(base, shift, own_x, ends, own, before, *filled)


def exact(a, b):
    return jnp.dot(a, b, precision=HI, preferred_element_type=F32)


def exact_t(a, b):
    dims = (((1,), (1,)), ((), ()))
    return lax.dot_general(a, b, dims, precision=HI, preferred_element_type=F32)


def precondition(jump, gram_x, gram_y, stiff):
    seen = exact(exact(gram_y, jump), gram_x)
    search = stiff * seen
    image = exact(exact(gram_y, search), gram_x)
    return search, image, jnp.sum(seen * search), jnp.sum(image * search)


def step_length(sums):
    return sums[0:1, 0:1] / (sums[1:2, 0:1] + 1e-06)


def scalars_block(upper, lower):
    at = lax.broadcasted_iota(jnp.int32, (8, N), 0)
    return jnp.where(at == 0, upper, jnp.where(at == 1, lower, 0.0))


def chain0_kernel(weight, jumps, gram_x, gram_y, stiff, own_x, basis_y, rows, image):
    search, image[0:N], upper, lower = precondition(
        jumps[:, 0].reshape(N, N), gram_x[...], gram_y[...], weight[...] * stiff[...].T
    )
    image[N : N + 8] = scalars_block(upper, lower)
    rows[...] = exact_t(exact_t(own_x[...], search), basis_y[...])


def chain0(*args):
    return pl.pallas_call(
        chain0_kernel,
        out_shape=(
            jax.ShapeDtypeStruct((ROWS, N), F32),
            jax.ShapeDtypeStruct((N + 8, N), F32),
        ),
        compiler_params=params(),
        cost_estimate=pl.CostEstimate(
            flops=N**3, bytes_accessed=N * N, transcendentals=0
        ),
        name="chain0",
    )(*args)


def chain1_kernel(
    ratio, weight, sums_in, jumps, image, before, after, pieces, gram_x, gram_y, stiff, own_x, basis_y, sums, out, rows
):
    alpha = step_length(sums_in[...])
    t = image[0:N]
    table = [pieces[:, 2 + pair].reshape(N, N) for pair in range(3)]
    own = table[1] * before[0:N] - table[0] * t
    other = table[2] * t - table[1] * after[0:N]
    q = jumps[:, 1].reshape(N, N) + alpha * (own - ratio[...] * other)
    search, _, upper, lower = precondition(
        q, gram_x[...], gram_y[...], weight[...] * stiff[...].T
    )
    sums[...] = scalars_block(upper, lower)
    out[...] = exact_t(exact_t(own_x[...], q), basis_y[...])
    rows[...] = exact_t(exact_t(own_x[...], search), basis_y[...])


def chain1(*args):
    return pl.pallas_call(
        chain1_kernel,
        out_shape=(
            jax.ShapeDtypeStruct((8, N), F32),
            jax.ShapeDtypeStruct((ROWS, N), F32),
            jax.ShapeDtypeStruct((ROWS, N), F32),
        ),
        compiler_params=params(),
        cost_estimate=pl.CostEstimate(
            flops=N**3, bytes_accessed=N * N, transcendentals=0
        ),
        name="chain1",
    )(*args)


def gram_kernel(basis_x, basis_y, gram_x, gram_y):
    gram_x[...] = exact(basis_x[...].T, basis_x[...])
    gram_y[...] = exact(basis_y[...].T, basis_y[...])


def grams(basis_x, basis_y):
    face = jax.ShapeDtypeStruct((N, N), F32)
    return pl.pallas_call(
        gram_kernel, out_shape=(face, face), compiler_params=params(), name="grams"
    )(basis_x, basis_y)


def from_behind(block, axis, distance):
    count = lax.axis_size(axis)
    route = [((i - distance) % count, i) for i in range(count)]
    return lax.ppermute(block, axis, route)


def from_partner(sums, bits):
    return lax.ppermute(sums, "sub", [(i, i ^ bits) for i in range(8)])


def over_pair(sums):
    return sums + from_partner(sums, 1)


def over_pairs(sums):
    return (sums + from_partner(sums, 2)) + (from_partner(sums, 4) + from_partner(sums, 6))


def exchange(block):
    return lax.all_to_all(block, "slab", split_axis=0, concat_axis=0, tiled=True)


def on_device(
    source, coarse, rho, basis_x, basis_y, basis_z, eigen_x, eigen_y, eigen_z, face_stiff
):
    source = source[0]
    sub_index = lax.axis_index("sub")
    slab_index = lax.axis_index("slab")
    subs = lax.axis_size("sub")
    own_rho = lax.dynamic_slice_in_dim(rho, sub_index, 1, 0)[0]
    next_rho = lax.dynamic_slice_in_dim(rho, (sub_index + 1) % subs, 1, 0)[0]
    weight = 0.5 * (own_rho + next_rho)
    start = slab_index * ROWS
    own_x = lax.dynamic_slice_in_dim(basis_x, start, ROWS, 0)

    part1 = forward(source, coarse, 1, basis_y, basis_z)
    lines = exchange(part1)

    shift = own_rho * eigen_y
    own_shift = lax.dynamic_slice_in_dim(shift, start, ROWS, 0)
    base_xz = own_rho * (eigen_x[:, None] + eigen_z[None, :])
    ends = jnp.stack([basis_z[0], basis_z[N - 1]])
    gram_x, gram_y = grams(basis_x, basis_y)

    part0 = forward(source, coarse, 0, basis_y, basis_z)
    pieces, near = faces(
        own_rho.reshape(1), shift, eigen_x[None], eigen_z[None], own_x, basis_z, part0, part1
    )
    shares = pieces[:, 0:2] - from_behind(near, "sub", -1)
    shares, lines, gram_x, gram_y, base_xz, ends = lax.optimization_barrier(
        (shares, lines, gram_x, gram_y, base_xz, ends)
    )
    spread = middle(base_xz, own_shift, basis_x, lines)
    shares = exchange(shares)
    shares, spread = lax.optimization_barrier((shares, spread))
    own_jumps = jnp.sum(shares, axis=0)
    jumps = exchange(jnp.broadcast_to(own_jumps[None], (SLABS,) + own_jumps.shape))
    spread, jumps = lax.optimization_barrier((spread, jumps))
    spread = exchange(spread)

    first, image0 = chain0(
        weight.reshape(1, 1), jumps, gram_x, gram_y, face_stiff, own_x, basis_y
    )
    before = from_behind(image0, "sub", 1)
    after = from_behind(image0, "sub", -1)

    terms = functools.partial(extra, base=base_xz, shift=shift, own_x=own_x, ends=ends)
    sums0 = image0[N:] + before[N:]
    before, sums0 = lax.optimization_barrier((before, sums0))
    more = terms(0, own=image0, before=before)
    sums0, more = lax.optimization_barrier((over_pairs(sums0), more))

    sums1, jump, change = chain1(
        (own_rho / next_rho).reshape(1, 1),
        weight.reshape(1, 1),
        sums0,
        jumps,
        image0,
        before,
        after,
        pieces,
        gram_x,
        gram_y,
        face_stiff,
        own_x,
        basis_y,
    )
    sums1, more = lax.optimization_barrier((sums1, more))
    more = terms(1, own=image0, before=before, filled=(more,))
    sums1, more = lax.optimization_barrier((over_pair(sums1), more))
    more = terms(2, own=image0, before=before, filled=(more,))
    sums1, more = lax.optimization_barrier((over_pairs(sums1), more))
    solution, multipliers = backward(
        sums0, sums1, first, change, spread, more, basis_y, basis_z
    )
    return (solution[None], multipliers[None], jump[None])


def solution(mesh):
    in_specs = (
        P("sub", "slab", None, None),
        P(None, "sub", "slab", None, None),
        P(),
        P(),
        P(),
        P(),
        P(),
        P(),
        P(),
        P(),
    )
    out_specs = (P("sub", "slab", None, None), P("sub", "slab", None), P("sub", "slab", None))
    return jax.shard_map(
        on_device, mesh=mesh, in_specs=in_specs, out_specs=out_specs, check_vma=False
    )
```

```python
import functools

import jax
import jax.numpy as jnp
from jax import lax
from jax.experimental import pallas as pl
from jax.experimental.pallas import tpu as pltpu
from jax.sharding import PartitionSpec as P

HI = lax.Precision.HIGHEST
F32 = jnp.float32
BF16 = jnp.bfloat16
VMEM_LIMIT = 60 * 1024 * 1024
N = 256
ROWS = 16
SLABS = 16
LANES = 128
GROUP = 8
PARTS = ((0, 6), (6, 11), (11, 16))
BLOCK_COST = 15 * 10**8
FIELD = (SLABS, 2, N // SLABS, ROWS, LANES)


def params():
    return pltpu.CompilerParams(vmem_limit_bytes=VMEM_LIMIT)


def split(a):
    high = a.astype(BF16)
    low = (a - high.astype(F32)).astype(BF16)
    return high, low


def dot(a, b):
    return jnp.dot(a, b, preferred_element_type=F32)


def dot3(a, b):
    return dot(a[0], b[0]) + (dot(a[0], b[1]) + dot(a[1], b[0]))


def put_split(scratch, a):
    scratch[0], scratch[1] = split(a)


def whole(shape):
    return pl.BlockSpec(shape, lambda *_: (0,) * len(shape))


def smem():
    return pl.BlockSpec(memory_space=pltpu.SMEM)


def forward_kernel(source, coarse, basis_y, basis_z, out, left, right):
    step = pl.program_id(0)

    @pl.when(step == 0)
    def _():
        put_split(left, basis_y[...].T)
        put_split(right, basis_z[...])

    load = (source[...] + coarse[0, 0]).reshape(GROUP * N, N)
    first = dot3(split(load), right)
    for x in range(GROUP):
        part = dot3(left, split(first[x * N : x * N + N]))
        at = pl.ds((step * GROUP + x) % 8, ROWS, stride=8)
        for slab in range(SLABS):
            for half in range(2):
                rows = out.at[slab, half].reshape(ROWS * 8, LANES)
                piece = part[slab * ROWS : slab * ROWS + ROWS, LANES * half : LANES * half + LANES]
                rows[at, :] = piece


def forward(source, coarse, step, basis_y, basis_z):
    return pl.pallas_call(
        forward_kernel,
        grid=(ROWS // GROUP,),
        in_specs=[
            pl.BlockSpec((GROUP, N, N), lambda x: (x, 0, 0)),
            pl.BlockSpec((1, 1, GROUP, N, N), lambda x: (step, 0, x, 0, 0)),
            whole((N, N)),
            whole((N, N)),
        ],
        out_specs=pl.BlockSpec(
            (SLABS, 2, ROWS, 8, LANES), lambda x: (0, 0, 0, x * GROUP // 8, 0)
        ),
        out_shape=jax.ShapeDtypeStruct(FIELD, F32),
        scratch_shapes=[pltpu.VMEM((2, N, N), BF16), pltpu.VMEM((2, N, N), BF16)],
        compiler_params=params(),
        cost_estimate=pl.CostEstimate(
            flops=12 * ROWS * N**3, bytes_accessed=12 * ROWS * N * N, transcendentals=0
        ),
        name="forward",
    )(source, coarse, basis_y, basis_z)


def middle_kernel(base, shift, basis_x, lines, out, left, right):
    step = pl.program_id(0)

    @pl.when(step == 0)
    def _():
        put_split(left, basis_x[...].T)
        put_split(right, basis_x[...])

    for j in range(GROUP):
        halves = [lines[:, half, j].reshape(N, LANES) for half in range(2)]
        field = jnp.concatenate(halves, axis=1)
        modes = dot3(left, split(field)) / (base[...] + shift[step * GROUP + j])
        spread = dot3(right, split(modes))
        for half in range(2):
            piece = spread[:, LANES * half : LANES * half + LANES]
            out[:, half, j] = piece.reshape(SLABS, ROWS, LANES)


def middle(base, shift, basis_x, lines):
    block = pl.BlockSpec((SLABS, 2, GROUP, ROWS, LANES), lambda j: (0, 0, j, 0, 0))
    return pl.pallas_call(
        middle_kernel,
        grid=(N // SLABS // GROUP,),
        in_specs=[whole((N, N)), smem(), whole((N, N)), block],
        out_specs=block,
        out_shape=jax.ShapeDtypeStruct(FIELD, F32),
        scratch_shapes=[pltpu.VMEM((2, N, N), BF16), pltpu.VMEM((2, N, N), BF16)],
        compiler_params=params(),
        cost_estimate=pl.CostEstimate(
            flops=12 * ROWS * N**3, bytes_accessed=8 * ROWS * N * N, transcendentals=0
        ),
        name="middle",
    )(base, shift, basis_x, lines)


def backward_kernel(
    sums0, sums1, first, change, field, extra, basis_y, basis_z, out, multipliers, left, right
):
    step = pl.program_id(0)
    alpha = step_length(sums0[...])

    @pl.when(step == 0)
    def _():
        multipliers[...] = alpha * first[...] + step_length(sums1[...]) * change[...]
        put_split(left, basis_y[...])
        put_split(right, basis_z[...].T)

    def total(x, slab, half):
        at = pl.ds((step * GROUP + x) % 8, ROWS, stride=8)
        terms = [ref.at[slab, half].reshape(ROWS * 8, LANES)[at, :] for ref in (field, extra)]
        return terms[0] + alpha * terms[1]

    parts = []
    for x in range(GROUP):
        halves = [
            jnp.concatenate([total(x, slab, half) for slab in range(SLABS)], axis=0)
            for half in range(2)
        ]
        parts.append(dot3(left, split(jnp.concatenate(halves, axis=1))))
    part = jnp.concatenate(parts, axis=0)
    out[...] = dot3(split(part), right).reshape(GROUP, N, N)


def backward(sums0, sums1, first, change, field, extra, basis_y, basis_z):
    block = pl.BlockSpec((SLABS, 2, ROWS, 8, LANES), lambda x: (0, 0, 0, x * GROUP // 8, 0))
    return pl.pallas_call(
        backward_kernel,
        grid=(ROWS // GROUP,),
        in_specs=[
            whole((8, 128)),
            whole((8, 128)),
            whole((ROWS, N)),
            whole((ROWS, N)),
            block,
            block,
            whole((N, N)),
            whole((N, N)),
        ],
        out_specs=[pl.BlockSpec((GROUP, N, N), lambda x: (x, 0, 0)), whole((ROWS, N))],
        out_shape=[
            jax.ShapeDtypeStruct((ROWS, N, N), F32),
            jax.ShapeDtypeStruct((ROWS, N), F32),
        ],
        scratch_shapes=[pltpu.VMEM((2, N, N), BF16), pltpu.VMEM((2, N, N), BF16)],
        compiler_params=params(),
        cost_estimate=pl.CostEstimate(
            flops=12 * ROWS * N**3, bytes_accessed=12 * ROWS * N * N, transcendentals=0
        ),
        name="backward",
    )(sums0, sums1, first, change, field, extra, basis_y, basis_z)


def inverse_parts(denom):
    high = pl.reciprocal(denom, approx=True).astype(BF16)
    wide = high.astype(F32)
    low = (wide * (1.0 - denom * wide)).astype(BF16)
    return high, low


def times_inverse(rows, denom):
    high, low = split(rows)
    count = rows.shape[0]
    w_high, w_low = inverse_parts(denom)
    both = dot(jnp.concatenate([high, low], axis=0), w_high)
    return both[:count] + (both[count:] + dot(high, w_low))


def faces_kernel(
    own_rho, shift, eigen_x, eigen_z, own_x, basis_z, part0, part1, out, near, base, products
):
    block = pl.program_id(0)
    first, last = basis_z[0:1], basis_z[N - 1 : N]

    @pl.when(block == 0)
    def _():
        rows = jnp.broadcast_to(eigen_z[...], (N, N)).T
        base[...] = own_rho[0] * (rows + eigen_x[...])
        at = lax.broadcasted_iota(jnp.int32, (16, N), 0)
        products[...] = jnp.where(
            at == 0,
            last * last,
            jnp.where(at == 1, last * first, jnp.where(at == 2, first * first, 0.0)),
        )

    for jj in range(ROWS):
        a = jnp.concatenate([part0[0, 0, jj], part0[0, 1, jj]], axis=1)
        b = jnp.concatenate([part1[0, 0, jj], part1[0, 1, jj]], axis=1)
        rows = jnp.concatenate([a * last, b * last, a * first, b * first, products[...]], axis=0)
        result = dot3(split(rows), inverse_parts(base[...] + shift[block * ROWS + jj]))
        sums = [
            jnp.sum(result[16 * face : 16 * face + 16] * own_x[...], axis=0, keepdims=True)
            for face in range(4)
        ]
        for load in range(2):
            out[0, load, jj : jj + 1] = sums[load]
            near[0, load, jj : jj + 1] = sums[2 + load]
        for pair in range(3):
            out[0, 2 + pair, jj : jj + 1] = result[64 + pair : 65 + pair]


def faces(own_rho, shift, eigen_x, eigen_z, own_x, basis_z, part0, part1):
    block = pl.BlockSpec((1, 2, ROWS, ROWS, LANES), lambda j: (j, 0, 0, 0, 0))
    return pl.pallas_call(
        faces_kernel,
        grid=(SLABS,),
        in_specs=[
            smem(),
            smem(),
            whole((1, N)),
            whole((1, N)),
            whole((ROWS, N)),
            whole((N, N)),
            block,
            block,
        ],
        out_specs=[
            pl.BlockSpec((1, 5, ROWS, N), lambda j: (j, 0, 0, 0)),
            pl.BlockSpec((1, 2, ROWS, N), lambda j: (j, 0, 0, 0)),
        ],
        out_shape=[
            jax.ShapeDtypeStruct((SLABS, 5, ROWS, N), F32),
            jax.ShapeDtypeStruct((SLABS, 2, ROWS, N), F32),
        ],
        scratch_shapes=[pltpu.VMEM((N, N), F32), pltpu.VMEM((16, N), F32)],
        compiler_params=params(),
        cost_estimate=pl.CostEstimate(flops=N**3, bytes_accessed=N * N, transcendentals=0),
        name="faces",
    )(own_rho, shift, eigen_x, eigen_z, own_x, basis_z, part0, part1)


def extra_kernel(part, base, shift, own_x, ends, own, before, *refs):
    out = refs[-1]
    block = PARTS[part][0] + pl.program_id(0)
    first, last = ends[0:1], ends[1:2]
    for jj in range(ROWS):
        upper = own_x[...] * own[jj : jj + 1]
        lower = own_x[...] * before[jj : jj + 1]
        rows = jnp.concatenate([upper, lower], axis=0)
        result = times_inverse(rows, base[...] + shift[block * ROWS + jj])
        result = first * result[16:] - last * result[:16]
        for half in range(2):
            out[0, half, jj] = result[:, LANES * half : LANES * half + LANES]


def extra(part, base, shift, own_x, ends, own, before, filled=()):
    skip, stop = PARTS[part]
    return pl.pallas_call(
        functools.partial(extra_kernel, part),
        grid=(stop - skip,),
        in_specs=[
            whole((N, N)),
            smem(),
            whole((ROWS, N)),
            whole((2, N)),
            pl.BlockSpec((ROWS, N), lambda j: (skip + j, 0)),
            pl.BlockSpec((ROWS, N), lambda j: (skip + j, 0)),
        ]
        + [pl.BlockSpec(memory_space=pl.ANY)] * len(filled),
        out_specs=pl.BlockSpec((1, 2, ROWS, ROWS, LANES), lambda j: (skip + j, 0, 0, 0, 0)),
        out_shape=jax.ShapeDtypeStruct(FIELD, F32),
        input_output_aliases={6: 0} if filled else {},
        compiler_params=params(),
        cost_estimate=pl.CostEstimate(
            flops=BLOCK_COST * (stop - skip), bytes_accessed=N * N, transcendentals=0
        ),
        name=f"extra{part}",
    )(base, shift, own_x, ends, own, before, *filled)


def exact(a, b):
    return jnp.dot(a, b, precision=HI, preferred_element_type=F32)


def exact_t(a, b):
    dims = (((1,), (1,)), ((), ()))
    return lax.dot_general(a, b, dims, precision=HI, preferred_element_type=F32)


def precondition(jump, gram_x, gram_y, stiff):
    seen = exact(exact(gram_y, jump), gram_x)
    search = stiff * seen
    image = exact(exact(gram_y, search), gram_x)
    return search, image, jnp.sum(seen * search), jnp.sum(image * search)


def step_length(sums):
    return sums[0:1, 0:1] / (sums[1:2, 0:1] + 1e-06)


def scalars_block(upper, lower):
    at = lax.broadcasted_iota(jnp.int32, (8, 128), 0)
    return jnp.where(at == 0, upper, jnp.where(at == 1, lower, 0.0))


def chain0_kernel(scale, jumps, gram_x, gram_y, stiff, own_x, basis_y, rows, image, sums):
    search, image[...], upper, lower = precondition(
        jumps[:, 0].reshape(N, N), gram_x[...], gram_y[...], scale[0] * stiff[...].T
    )
    sums[...] = scalars_block(upper, lower)
    rows[...] = exact_t(exact_t(own_x[...], search), basis_y[...])


def chain0(*args):
    face = jax.ShapeDtypeStruct((N, N), F32)
    return pl.pallas_call(
        chain0_kernel,
        in_specs=[smem()] + [pl.BlockSpec(memory_space=pltpu.VMEM)] * 6,
        out_shape=(jax.ShapeDtypeStruct((ROWS, N), F32), face, jax.ShapeDtypeStruct((8, 128), F32)),
        compiler_params=params(),
        cost_estimate=pl.CostEstimate(
            flops=N**3, bytes_accessed=N * N, transcendentals=0
        ),
        name="chain0",
    )(*args)


def chain1_kernel(
    scale, sums_in, jumps, image, before, after, pieces, gram_x, gram_y, stiff, own_x, basis_y, sums, out, rows
):
    alpha, ratio, weight = step_length(sums_in[...]), scale[0], scale[1]
    t = image[...]
    table = [pieces[:, 2 + pair].reshape(N, N) for pair in range(3)]
    own = table[1] * before[...] - table[0] * t
    other = table[2] * t - table[1] * after[...]
    q = jumps[:, 1].reshape(N, N) + alpha * (own - ratio * other)
    search, _, upper, lower = precondition(
        q, gram_x[...], gram_y[...], weight * stiff[...].T
    )
    sums[...] = scalars_block(upper, lower)
    out[...] = exact_t(exact_t(own_x[...], q), basis_y[...])
    rows[...] = exact_t(exact_t(own_x[...], search), basis_y[...])


def chain1(*args):
    return pl.pallas_call(
        chain1_kernel,
        in_specs=[smem()] + [pl.BlockSpec(memory_space=pltpu.VMEM)] * 11,
        out_shape=(
            jax.ShapeDtypeStruct((8, 128), F32),
            jax.ShapeDtypeStruct((ROWS, N), F32),
            jax.ShapeDtypeStruct((ROWS, N), F32),
        ),
        compiler_params=params(),
        cost_estimate=pl.CostEstimate(
            flops=N**3, bytes_accessed=N * N, transcendentals=0
        ),
        name="chain1",
    )(*args)


def gram_kernel(basis_x, basis_y, gram_x, gram_y):
    gram_x[...] = exact(basis_x[...].T, basis_x[...])
    gram_y[...] = exact(basis_y[...].T, basis_y[...])


def grams(basis_x, basis_y):
    face = jax.ShapeDtypeStruct((N, N), F32)
    return pl.pallas_call(
        gram_kernel, out_shape=(face, face), compiler_params=params(), name="grams"
    )(basis_x, basis_y)


def from_behind(block, axis, distance):
    count = lax.axis_size(axis)
    route = [((i - distance) % count, i) for i in range(count)]
    return lax.ppermute(block, axis, route)


def from_partner(sums, bits):
    return lax.ppermute(sums, "sub", [(i, i ^ bits) for i in range(8)])


def over_pair(sums):
    return sums + from_partner(sums, 1)


def over_pairs(sums):
    return (sums + from_partner(sums, 2)) + (from_partner(sums, 4) + from_partner(sums, 6))


def exchange(block):
    return lax.all_to_all(block, "slab", split_axis=0, concat_axis=0, tiled=True)


def on_device(
    source, coarse, rho, basis_x, basis_y, basis_z, eigen_x, eigen_y, eigen_z, face_stiff
):
    source = source[0]
    sub_index = lax.axis_index("sub")
    slab_index = lax.axis_index("slab")
    subs = lax.axis_size("sub")
    own_rho = lax.dynamic_slice_in_dim(rho, sub_index, 1, 0)[0]
    next_rho = lax.dynamic_slice_in_dim(rho, (sub_index + 1) % subs, 1, 0)[0]
    weight = 0.5 * (own_rho + next_rho)
    start = slab_index * ROWS
    own_x = lax.dynamic_slice_in_dim(basis_x, start, ROWS, 0)

    near_x = from_behind(eigen_x, "slab", 1)
    near_z = from_behind(eigen_z, "slab", 4)
    near_y = from_behind(eigen_y, "slab", -1)
    far_x = from_behind(eigen_x, "slab", -4)
    part1 = forward(source, coarse, 1, basis_y, basis_z)
    near_x, near_y, near_z, far_x, part1 = lax.optimization_barrier(
        (near_x, near_y, near_z, far_x, part1)
    )
    lines = exchange(part1)

    shift = own_rho * near_y
    own_shift = lax.dynamic_slice_in_dim(shift, start, ROWS, 0)
    base_xz = own_rho * (far_x[:, None] + eigen_z[None, :])
    ends = jnp.stack([basis_z[0], basis_z[N - 1]])
    gram_x, gram_y = grams(basis_x, basis_y)

    part0 = forward(source, coarse, 0, basis_y, basis_z)
    pieces, near = faces(
        own_rho.reshape(1), shift, near_x[None], near_z[None], own_x, basis_z, part0, part1
    )
    shares = pieces[:, 0:2] - from_behind(near, "sub", -1)
    shares, lines, gram_x, gram_y, base_xz, ends = lax.optimization_barrier(
        (shares, lines, gram_x, gram_y, base_xz, ends)
    )
    spread = middle(base_xz, own_shift, basis_x, lines)
    shares = exchange(shares)
    shares, spread = lax.optimization_barrier((shares, spread))
    own_jumps = jnp.sum(shares, axis=0)
    jumps = exchange(jnp.broadcast_to(own_jumps[None], (SLABS,) + own_jumps.shape))
    spread, jumps = lax.optimization_barrier((spread, jumps))
    spread = exchange(spread)

    first, image0, sums0 = chain0(
        weight.reshape(1), jumps, gram_x, gram_y, face_stiff, own_x, basis_y
    )
    before = from_behind(image0, "sub", 1)
    after = from_behind(image0, "sub", -1)

    terms = functools.partial(extra, base=base_xz, shift=shift, own_x=own_x, ends=ends)
    sums0 = over_pair(sums0)
    before, sums0 = lax.optimization_barrier((before, sums0))
    more = terms(0, own=image0, before=before)
    sums0, more = lax.optimization_barrier((over_pairs(sums0), more))

    scale = jnp.stack([own_rho / next_rho, weight])
    sums1, jump, change = chain1(
        scale,
        sums0,
        jumps,
        image0,
        before,
        after,
        pieces,
        gram_x,
        gram_y,
        face_stiff,
        own_x,
        basis_y,
    )
    sums1, more = lax.optimization_barrier((sums1, more))
    more = terms(1, own=image0, before=before, filled=(more,))
    sums1, more = lax.optimization_barrier((over_pair(sums1), more))
    more = terms(2, own=image0, before=before, filled=(more,))
    sums1, more = lax.optimization_barrier((over_pairs(sums1), more))
    solution, multipliers = backward(
        sums0, sums1, first, change, spread, more, basis_y, basis_z
    )
    return (solution[None], multipliers[None], jump[None])


def solution(mesh):
    in_specs = (
        P("sub", "slab", None, None),
        P(None, "sub", "slab", None, None),
        P(),
        P(),
        P(),
        P(),
        P(),
        P(),
        P(),
        P(),
    )
    out_specs = (P("sub", "slab", None, None), P("sub", "slab", None), P("sub", "slab", None))
    return jax.shard_map(
        on_device, mesh=mesh, in_specs=in_specs, out_specs=out_specs, check_vma=False
    )
```

```python
import functools

import jax
import jax.numpy as jnp
from jax import lax
from jax.experimental import pallas as pl
from jax.experimental.pallas import tpu as pltpu
from jax.sharding import PartitionSpec as P

HI = lax.Precision.HIGHEST
F32 = jnp.float32
BF16 = jnp.bfloat16
VMEM_LIMIT = 60 * 1024 * 1024
N = 256
ROWS = 16
SLABS = 16
LANES = 128
GROUP = 8
PARTS = ((0, 6), (6, 11), (11, 16))
BLOCK_COST = 15 * 10**8
FIELD = (SLABS, 2, N // SLABS, ROWS, LANES)


def params():
    return pltpu.CompilerParams(vmem_limit_bytes=VMEM_LIMIT)


def split(a):
    high = a.astype(BF16)
    low = (a - high.astype(F32)).astype(BF16)
    return high, low


def dot(a, b):
    return jnp.dot(a, b, preferred_element_type=F32)


def dot3(a, b):
    return dot(a[0], b[0]) + (dot(a[0], b[1]) + dot(a[1], b[0]))


def put_split(scratch, a):
    scratch[0], scratch[1] = split(a)


def whole(shape):
    return pl.BlockSpec(shape, lambda *_: (0,) * len(shape))


def smem():
    return pl.BlockSpec(memory_space=pltpu.SMEM)


def forward_kernel(source, coarse, basis_y, basis_z, out, left, right):
    step = pl.program_id(0)

    @pl.when(step == 0)
    def _():
        put_split(left, basis_y[...].T)
        put_split(right, basis_z[...])

    load = (source[...] + coarse[0, 0]).reshape(GROUP * N, N)
    first = dot3(split(load), right)
    for x in range(GROUP):
        part = dot3(left, split(first[x * N : x * N + N]))
        at = pl.ds((step * GROUP + x) % 8, ROWS, stride=8)
        for slab in range(SLABS):
            for half in range(2):
                rows = out.at[slab, half].reshape(ROWS * 8, LANES)
                piece = part[slab * ROWS : slab * ROWS + ROWS, LANES * half : LANES * half + LANES]
                rows[at, :] = piece


def forward(source, coarse, step, basis_y, basis_z):
    return pl.pallas_call(
        forward_kernel,
        grid=(ROWS // GROUP,),
        in_specs=[
            pl.BlockSpec((GROUP, N, N), lambda x: (x, 0, 0)),
            pl.BlockSpec((1, 1, GROUP, N, N), lambda x: (step, 0, x, 0, 0)),
            whole((N, N)),
            whole((N, N)),
        ],
        out_specs=pl.BlockSpec(
            (SLABS, 2, ROWS, 8, LANES), lambda x: (0, 0, 0, x * GROUP // 8, 0)
        ),
        out_shape=jax.ShapeDtypeStruct(FIELD, F32),
        scratch_shapes=[pltpu.VMEM((2, N, N), BF16), pltpu.VMEM((2, N, N), BF16)],
        compiler_params=params(),
        cost_estimate=pl.CostEstimate(
            flops=12 * ROWS * N**3, bytes_accessed=12 * ROWS * N * N, transcendentals=0
        ),
        name="forward",
    )(source, coarse, basis_y, basis_z)


def middle_kernel(base, shift, basis_x, lines, out, left, right):
    step = pl.program_id(0)

    @pl.when(step == 0)
    def _():
        put_split(left, basis_x[...].T)
        put_split(right, basis_x[...])

    for j in range(GROUP):
        halves = [lines[:, half, j].reshape(N, LANES) for half in range(2)]
        field = jnp.concatenate(halves, axis=1)
        modes = dot3(left, split(field)) / (base[...] + shift[step * GROUP + j])
        spread = dot3(right, split(modes))
        for half in range(2):
            piece = spread[:, LANES * half : LANES * half + LANES]
            out[:, half, j] = piece.reshape(SLABS, ROWS, LANES)


def middle(base, shift, basis_x, lines):
    block = pl.BlockSpec((SLABS, 2, GROUP, ROWS, LANES), lambda j: (0, 0, j, 0, 0))
    return pl.pallas_call(
        middle_kernel,
        grid=(N // SLABS // GROUP,),
        in_specs=[whole((N, N)), smem(), whole((N, N)), block],
        out_specs=block,
        out_shape=jax.ShapeDtypeStruct(FIELD, F32),
        scratch_shapes=[pltpu.VMEM((2, N, N), BF16), pltpu.VMEM((2, N, N), BF16)],
        compiler_params=params(),
        cost_estimate=pl.CostEstimate(
            flops=12 * ROWS * N**3, bytes_accessed=8 * ROWS * N * N, transcendentals=0
        ),
        name="middle",
    )(base, shift, basis_x, lines)


def backward_kernel(
    sums0, sums1, first, change, field, extra, basis_y, basis_z, out, multipliers, left, right
):
    step = pl.program_id(0)
    alpha = step_length(sums0[...])

    @pl.when(step == 0)
    def _():
        multipliers[...] = alpha * first[...] + step_length(sums1[...]) * change[...]
        put_split(left, basis_y[...])
        put_split(right, basis_z[...].T)

    def total(x, slab, half):
        at = pl.ds((step * GROUP + x) % 8, ROWS, stride=8)
        terms = [ref.at[slab, half].reshape(ROWS * 8, LANES)[at, :] for ref in (field, extra)]
        return terms[0] + alpha * terms[1]

    parts = []
    for x in range(GROUP):
        halves = [
            jnp.concatenate([total(x, slab, half) for slab in range(SLABS)], axis=0)
            for half in range(2)
        ]
        parts.append(dot3(left, split(jnp.concatenate(halves, axis=1))))
    part = jnp.concatenate(parts, axis=0)
    out[...] = dot3(split(part), right).reshape(GROUP, N, N)


def backward(sums0, sums1, first, change, field, extra, basis_y, basis_z):
    block = pl.BlockSpec((SLABS, 2, ROWS, 8, LANES), lambda x: (0, 0, 0, x * GROUP // 8, 0))
    return pl.pallas_call(
        backward_kernel,
        grid=(ROWS // GROUP,),
        in_specs=[
            whole((8, 128)),
            whole((8, 128)),
            whole((ROWS, N)),
            whole((ROWS, N)),
            block,
            block,
            whole((N, N)),
            whole((N, N)),
        ],
        out_specs=[pl.BlockSpec((GROUP, N, N), lambda x: (x, 0, 0)), whole((ROWS, N))],
        out_shape=[
            jax.ShapeDtypeStruct((ROWS, N, N), F32),
            jax.ShapeDtypeStruct((ROWS, N), F32),
        ],
        scratch_shapes=[pltpu.VMEM((2, N, N), BF16), pltpu.VMEM((2, N, N), BF16)],
        compiler_params=params(),
        cost_estimate=pl.CostEstimate(
            flops=12 * ROWS * N**3, bytes_accessed=12 * ROWS * N * N, transcendentals=0
        ),
        name="backward",
    )(sums0, sums1, first, change, field, extra, basis_y, basis_z)


def inverse_parts(denom):
    high = pl.reciprocal(denom, approx=True).astype(BF16)
    wide = high.astype(F32)
    low = (wide * (1.0 - denom * wide)).astype(BF16)
    return high, low


def times_inverse(rows, denom):
    high, low = split(rows)
    count = rows.shape[0]
    w_high, w_low = inverse_parts(denom)
    both = dot(jnp.concatenate([high, low], axis=0), w_high)
    return both[:count] + (both[count:] + dot(high, w_low))


def faces_kernel(
    own_rho, shift, eigen_x, eigen_z, own_x, basis_z, part0, part1, out, near, base, products
):
    block = pl.program_id(0)
    first, last = basis_z[0:1], basis_z[N - 1 : N]

    @pl.when(block == 0)
    def _():
        rows = jnp.broadcast_to(eigen_z[...], (N, N)).T
        base[...] = own_rho[0] * (rows + eigen_x[...])
        at = lax.broadcasted_iota(jnp.int32, (16, N), 0)
        products[...] = jnp.where(
            at == 0,
            last * last,
            jnp.where(at == 1, last * first, jnp.where(at == 2, first * first, 0.0)),
        )

    for jj in range(ROWS):
        a = jnp.concatenate([part0[0, 0, jj], part0[0, 1, jj]], axis=1)
        b = jnp.concatenate([part1[0, 0, jj], part1[0, 1, jj]], axis=1)
        rows = jnp.concatenate([a * last, b * last, a * first, b * first, products[...]], axis=0)
        result = dot3(split(rows), inverse_parts(base[...] + shift[block * ROWS + jj]))
        sums = [
            jnp.sum(result[16 * face : 16 * face + 16] * own_x[...], axis=0, keepdims=True)
            for face in range(4)
        ]
        for load in range(2):
            out[0, load, jj : jj + 1] = sums[load]
            near[0, load, jj : jj + 1] = sums[2 + load]
        for pair in range(3):
            out[0, 2 + pair, jj : jj + 1] = result[64 + pair : 65 + pair]


def faces(own_rho, shift, eigen_x, eigen_z, own_x, basis_z, part0, part1):
    block = pl.BlockSpec((1, 2, ROWS, ROWS, LANES), lambda j: (j, 0, 0, 0, 0))
    return pl.pallas_call(
        faces_kernel,
        grid=(SLABS,),
        in_specs=[
            smem(),
            smem(),
            whole((1, N)),
            whole((1, N)),
            whole((ROWS, N)),
            whole((N, N)),
            block,
            block,
        ],
        out_specs=[
            pl.BlockSpec((1, 5, ROWS, N), lambda j: (j, 0, 0, 0)),
            pl.BlockSpec((1, 2, ROWS, N), lambda j: (j, 0, 0, 0)),
        ],
        out_shape=[
            jax.ShapeDtypeStruct((SLABS, 5, ROWS, N), F32),
            jax.ShapeDtypeStruct((SLABS, 2, ROWS, N), F32),
        ],
        scratch_shapes=[pltpu.VMEM((N, N), F32), pltpu.VMEM((16, N), F32)],
        compiler_params=params(),
        cost_estimate=pl.CostEstimate(flops=N**3, bytes_accessed=N * N, transcendentals=0),
        name="faces",
    )(own_rho, shift, eigen_x, eigen_z, own_x, basis_z, part0, part1)


def extra_kernel(part, base, shift, own_x, ends, own, before, *refs):
    out = refs[-1]
    block = PARTS[part][0] + pl.program_id(0)
    first, last = ends[0:1], ends[1:2]
    for jj in range(ROWS):
        upper = own_x[...] * own[jj : jj + 1]
        lower = own_x[...] * before[jj : jj + 1]
        rows = jnp.concatenate([upper, lower], axis=0)
        result = times_inverse(rows, base[...] + shift[block * ROWS + jj])
        result = first * result[16:] - last * result[:16]
        for half in range(2):
            out[0, half, jj] = result[:, LANES * half : LANES * half + LANES]


def extra(part, base, shift, own_x, ends, own, before, filled=()):
    skip, stop = PARTS[part]
    return pl.pallas_call(
        functools.partial(extra_kernel, part),
        grid=(stop - skip,),
        in_specs=[
            whole((N, N)),
            smem(),
            whole((ROWS, N)),
            whole((2, N)),
            pl.BlockSpec((ROWS, N), lambda j: (skip + j, 0)),
            pl.BlockSpec((ROWS, N), lambda j: (skip + j, 0)),
        ]
        + [pl.BlockSpec(memory_space=pl.ANY)] * len(filled),
        out_specs=pl.BlockSpec((1, 2, ROWS, ROWS, LANES), lambda j: (skip + j, 0, 0, 0, 0)),
        out_shape=jax.ShapeDtypeStruct(FIELD, F32),
        input_output_aliases={6: 0} if filled else {},
        compiler_params=params(),
        cost_estimate=pl.CostEstimate(
            flops=BLOCK_COST * (stop - skip), bytes_accessed=N * N, transcendentals=0
        ),
        name=f"extra{part}",
    )(base, shift, own_x, ends, own, before, *filled)


def exact(a, b):
    return jnp.dot(a, b, precision=HI, preferred_element_type=F32)


def exact_t(a, b):
    dims = (((1,), (1,)), ((), ()))
    return lax.dot_general(a, b, dims, precision=HI, preferred_element_type=F32)


def precondition(jump, gram_x, gram_y, stiff):
    seen = exact(exact(gram_y, jump), gram_x)
    search = stiff * seen
    image = exact(exact(gram_y, search), gram_x)
    return search, image, jnp.sum(seen * search), jnp.sum(image * search)


def step_length(sums):
    return sums[0:1, 0:1] / (sums[1:2, 0:1] + 1e-06)


def scalars_block(upper, lower):
    at = lax.broadcasted_iota(jnp.int32, (8, 128), 0)
    return jnp.where(at == 0, upper, jnp.where(at == 1, lower, 0.0))


def chain0_kernel(scale, jumps, gram_x, gram_y, stiff, own_x, basis_y, rows, image, sums):
    search, image[...], upper, lower = precondition(
        jumps[:, 0].reshape(N, N), gram_x[...], gram_y[...], scale[0] * stiff[...].T
    )
    sums[...] = scalars_block(upper, lower)
    rows[...] = exact_t(exact_t(own_x[...], search), basis_y[...])


def chain0(*args):
    face = jax.ShapeDtypeStruct((N, N), F32)
    return pl.pallas_call(
        chain0_kernel,
        in_specs=[smem()] + [pl.BlockSpec(memory_space=pltpu.VMEM)] * 6,
        out_shape=(jax.ShapeDtypeStruct((ROWS, N), F32), face, jax.ShapeDtypeStruct((8, 128), F32)),
        compiler_params=params(),
        cost_estimate=pl.CostEstimate(
            flops=N**3, bytes_accessed=N * N, transcendentals=0
        ),
        name="chain0",
    )(*args)


def chain1_kernel(
    scale, sums_in, jumps, image, before, after, pieces, gram_x, gram_y, stiff, own_x, basis_y, sums, out, rows
):
    alpha, ratio, weight = step_length(sums_in[...]), scale[0], scale[1]
    t = image[...]
    table = [pieces[:, 2 + pair].reshape(N, N) for pair in range(3)]
    own = table[1] * before[...] - table[0] * t
    other = table[2] * t - table[1] * after[...]
    q = jumps[:, 1].reshape(N, N) + alpha * (own - ratio * other)
    search, _, upper, lower = precondition(
        q, gram_x[...], gram_y[...], weight * stiff[...].T
    )
    sums[...] = scalars_block(upper, lower)
    out[...] = exact_t(exact_t(own_x[...], q), basis_y[...])
    rows[...] = exact_t(exact_t(own_x[...], search), basis_y[...])


def chain1(*args):
    return pl.pallas_call(
        chain1_kernel,
        in_specs=[smem()] + [pl.BlockSpec(memory_space=pltpu.VMEM)] * 11,
        out_shape=(
            jax.ShapeDtypeStruct((8, 128), F32),
            jax.ShapeDtypeStruct((ROWS, N), F32),
            jax.ShapeDtypeStruct((ROWS, N), F32),
        ),
        compiler_params=params(),
        cost_estimate=pl.CostEstimate(
            flops=N**3, bytes_accessed=N * N, transcendentals=0
        ),
        name="chain1",
    )(*args)


def gram_kernel(basis_x, basis_y, gram_x, gram_y):
    gram_x[...] = exact(basis_x[...].T, basis_x[...])
    gram_y[...] = exact(basis_y[...].T, basis_y[...])


def grams(basis_x, basis_y):
    face = jax.ShapeDtypeStruct((N, N), F32)
    return pl.pallas_call(
        gram_kernel, out_shape=(face, face), compiler_params=params(), name="grams"
    )(basis_x, basis_y)


def from_behind(block, axis, distance):
    count = lax.axis_size(axis)
    route = [((i - distance) % count, i) for i in range(count)]
    return lax.ppermute(block, axis, route)


def from_partner(sums, bits):
    return lax.ppermute(sums, "sub", [(i, i ^ bits) for i in range(8)])


def over_pair(sums):
    return sums + from_partner(sums, 1)


def over_pairs(sums):
    return (sums + from_partner(sums, 2)) + (from_partner(sums, 4) + from_partner(sums, 6))


def exchange(block):
    return lax.all_to_all(block, "slab", split_axis=0, concat_axis=0, tiled=True)


def on_device(
    source, coarse, rho, basis_x, basis_y, basis_z, eigen_x, eigen_y, eigen_z, face_stiff
):
    source = source[0]
    sub_index = lax.axis_index("sub")
    slab_index = lax.axis_index("slab")
    subs = lax.axis_size("sub")
    own_rho = lax.dynamic_slice_in_dim(rho, sub_index, 1, 0)[0]
    next_rho = lax.dynamic_slice_in_dim(rho, (sub_index + 1) % subs, 1, 0)[0]
    weight = 0.5 * (own_rho + next_rho)
    start = slab_index * ROWS
    own_x = lax.dynamic_slice_in_dim(basis_x, start, ROWS, 0)

    near_x = from_behind(eigen_x, "slab", 1)
    near_z = from_behind(eigen_z, "slab", 4)
    part1 = forward(source, coarse, 1, basis_y, basis_z)
    near_x, near_z, part1 = lax.optimization_barrier((near_x, near_z, part1))
    lines = exchange(part1)

    shift = own_rho * eigen_y
    own_shift = lax.dynamic_slice_in_dim(shift, start, ROWS, 0)
    base_xz = own_rho * (eigen_x[:, None] + eigen_z[None, :])
    ends = jnp.stack([basis_z[0], basis_z[N - 1]])
    gram_x, gram_y = grams(basis_x, basis_y)

    part0 = forward(source, coarse, 0, basis_y, basis_z)
    pieces, near = faces(
        own_rho.reshape(1), shift, near_x[None], near_z[None], own_x, basis_z, part0, part1
    )
    shares = pieces[:, 0:2] - from_behind(near, "sub", -1)
    shares, lines, gram_x, gram_y, base_xz, ends = lax.optimization_barrier(
        (shares, lines, gram_x, gram_y, base_xz, ends)
    )
    spread = middle(base_xz, own_shift, basis_x, lines)
    shares = exchange(shares)
    shares, spread = lax.optimization_barrier((shares, spread))
    own_jumps = jnp.sum(shares, axis=0)
    jumps = exchange(jnp.broadcast_to(own_jumps[None], (SLABS,) + own_jumps.shape))
    spread, jumps = lax.optimization_barrier((spread, jumps))
    spread = exchange(spread)

    first, image0, sums0 = chain0(
        weight.reshape(1), jumps, gram_x, gram_y, face_stiff, own_x, basis_y
    )
    before = from_behind(image0, "sub", 1)
    after = from_behind(image0, "sub", -1)

    terms = functools.partial(extra, base=base_xz, shift=shift, own_x=own_x, ends=ends)
    sums0 = over_pair(sums0)
    before, sums0 = lax.optimization_barrier((before, sums0))
    more = terms(0, own=image0, before=before)
    sums0, more = lax.optimization_barrier((over_pairs(sums0), more))

    scale = jnp.stack([own_rho / next_rho, weight])
    sums1, jump, change = chain1(
        scale,
        sums0,
        jumps,
        image0,
        before,
        after,
        pieces,
        gram_x,
        gram_y,
        face_stiff,
        own_x,
        basis_y,
    )
    sums1, more = lax.optimization_barrier((sums1, more))
    more = terms(1, own=image0, before=before, filled=(more,))
    sums1, more = lax.optimization_barrier((over_pair(sums1), more))
    more = terms(2, own=image0, before=before, filled=(more,))
    sums1, more = lax.optimization_barrier((over_pairs(sums1), more))
    solution, multipliers = backward(
        sums0, sums1, first, change, spread, more, basis_y, basis_z
    )
    return (solution[None], multipliers[None], jump[None])


def solution(mesh):
    in_specs = (
        P("sub", "slab", None, None),
        P(None, "sub", "slab", None, None),
        P(),
        P(),
        P(),
        P(),
        P(),
        P(),
        P(),
        P(),
    )
    out_specs = (P("sub", "slab", None, None), P("sub", "slab", None), P("sub", "slab", None))
    return jax.shard_map(
        on_device, mesh=mesh, in_specs=in_specs, out_specs=out_specs, check_vma=False
    )
```
